256 devices in a mesh: seg: 32 (over x_hi, z, core), rad: 8 (over x_lo, y).
Axes of the slice: x: 4 (x_hi: 2, x_lo: 2; x = x_hi * 2 + x_lo), y: 4, z: 8, core: 2. Of those that a mesh axis runs over, the one named last changes fastest.
Arguments:
- start_vector: float32 [32, 3, 8, 384, 768], P('seg', None, 'rad'), may hold values from -12 to 12
- coupling: bfloat16 [32, 3, 3, 8, 384, 768], P('seg', None, None, 'rad'), may hold values from -1.796875 to 1.796875
- advect: float32 [8], P('rad'), may hold values from 0.001 to 0.004
Outputs:
- next_basis: float32 [32, 3, 8, 384, 768], P('seg', None, 'rad')
- hessenberg: float32 [6], replicated
The draws below stay inside these ranges and needn't reach their ends.
All inputs are finite; a program needn't handle non-finite values.
Results may differ from the reference program's by a relative error of at most 0.008.
Values may be sent and summed in bfloat16 or wider, within the bound.
A program may use at most 128 MiB of HBM per device.

```python
import math
import jax
import jax.numpy as jnp
from jax import lax

M = 384
K = 768
RADIAL_ALL = 256
WINDOW_START = 124
STEPS = 1
NR = 8
SEGS = 32


def draw_start_vector(key, part):
    k_noise, k_scale = jax.random.split(key, 2)
    seg_pos = jnp.arange(SEGS, dtype=jnp.float32) / max(SEGS - 1, 1)
    rad_pos = jnp.arange(NR, dtype=jnp.float32) / max(NR - 1, 1)
    jitter = jax.random.uniform(k_scale, (SEGS, 3, NR), jnp.float32)
    log_scale = math.log(3.0) * (seg_pos[:, None, None] + rad_pos[None, None, :] + jitter) - math.log(9.0)
    scaling = jnp.exp(log_scale)[..., None, None]
    noise_draw = jnp.clip(jax.random.normal(k_noise, (SEGS, 3, NR, M, K), jnp.float32), -4.0, 4.0)
    return (noise_draw * scaling).astype(jnp.float32)


def level_of(stream_key, shape, shards, smallest, largest):
    def one(axis_at, parts):
        steps = jax.random.uniform(jax.random.fold_in(jax.random.fold_in(stream_key, 6), axis_at), (parts,), jnp.float32, smallest / len(shards), largest / len(shards))
        return jnp.repeat(jnp.exp(steps), shape[axis_at] // parts).reshape((-1,) + (1,) * (len(shape) - axis_at - 1))

    level = one(*shards[0])
    for cut in shards[1:]:
        level = level * one(*cut)
    return level


def centred(own_key, dims, deviation, bound, cuts=(), kind=jnp.bfloat16):
    drawn = jax.random.normal(own_key, dims, jnp.float32) * deviation
    if len(cuts) > 0:
        drawn = level_of(own_key, dims, cuts, -0.22, 0.18) * drawn
    return jnp.clip(drawn, min=-bound, max=bound).astype(kind)


def setup_inputs(seed: int = 0) -> dict:
    keys = jax.random.split(jax.random.key(seed), 4)
    return {
        "start_vector": draw_start_vector(jax.random.fold_in(keys[3], 71), 0),
        "coupling": centred(keys[1], (SEGS, 3, 3, NR, M, K), 0.3, 1.796875, ((0, 32), (3, 8))),
        "advect": jnp.clip(jnp.exp(math.log(0.004) - 1.3862944 * jax.random.uniform(keys[2], (NR,), jnp.float32) ** level_of(keys[2], (NR,), ((0, 8),), -0.2, 0.2)), 0.001, 0.004),
    }


RADIAL_GAIN = 0.25
VISC_AXIAL = 4.0
VISC_TURN = 0.05

def make_tables(count):
    index = jnp.arange(count, dtype=jnp.int32)
    half_len = count // 2
    freq = jnp.where(index <= half_len, index, index - half_len)
    phase = freq[:, None] * index[None, :] % count
    angle = 2.0 * math.pi / count * phase.astype(jnp.float32)
    synth = jnp.where((index <= half_len)[:, None], jnp.cos(angle), jnp.sin(angle))
    weight = jnp.where((index == 0) | (index == half_len), 1.0 / count, 2.0 / count).astype(jnp.float32)
    analysis = weight[:, None] * synth
    return (synth.astype(jnp.bfloat16), analysis.astype(jnp.bfloat16), freq)

def make_divisor(radius_index, all_rows, freq_m, freq_k, modes_m, modes_k):
    radius = (radius_index.astype(jnp.float32) + 0.5) / all_rows
    axial = (freq_k.astype(jnp.float32) / (modes_k // 2)) ** 2
    turning = (freq_m.astype(jnp.float32) / (modes_m // 2)) ** 2
    return 1.0 + VISC_AXIAL * axial[None, None, :] + VISC_TURN * turning[None, :, None] / (radius * radius)[:, None, None]

def axial_derivative(field):
    half_len = field.shape[-1] // 2
    wavenum = jnp.arange(1, half_len, dtype=jnp.int32).astype(jnp.float32)
    zeros_col = jnp.zeros(field.shape[:-1] + (1,), jnp.float32)
    return jnp.concatenate([zeros_col, wavenum * field[..., half_len + 1:], zeros_col, -wavenum * field[..., 1:half_len]], axis=-1)

def tangent(field, couple, advect, tables, divisor):
    synth_m, anal_m, synth_k, anal_k = tables
    rounded = field.astype(jnp.bfloat16)
    section_one = jnp.einsum('crmk,kz->crmz', rounded.astype(jnp.float32), synth_k.astype(jnp.float32)).astype(jnp.bfloat16)
    physical = jnp.einsum('mt,crmz->crtz', synth_m.astype(jnp.float32), section_one.astype(jnp.float32))
    mixed = lax.optimization_barrier(jnp.sum(couple.astype(jnp.float32) * physical[None], axis=1)).astype(jnp.bfloat16)
    section_two = jnp.einsum('crtz,kz->crtk', mixed.astype(jnp.float32), anal_k.astype(jnp.float32)).astype(jnp.bfloat16)
    spectral = jnp.einsum('mt,crtk->crmk', anal_m.astype(jnp.float32), section_two.astype(jnp.float32))
    deriv = axial_derivative(field)
    padded = jnp.pad(rounded.astype(jnp.float32), ((0, 0), (1, 1), (0, 0), (0, 0)))
    radial = RADIAL_GAIN * (padded[:, 2:] - 2.0 * padded[:, 1:-1] + padded[:, :-2])
    return (field + spectral - advect[None, :, None, None] * deriv + radial) / divisor

def reference(start_vector, coupling, advect):
    synth_m, anal_m, freq_m = make_tables(M)
    synth_k, anal_k, freq_k = make_tables(K)
    tables = (synth_m, anal_m, synth_k, anal_k)
    radius_index = jnp.arange(NR, dtype=jnp.int32) + WINDOW_START
    divisor = make_divisor(radius_index, RADIAL_ALL, freq_m, freq_k, M, K)
    cells = float(SEGS * 3 * NR * M * K)

    def inner(left, right):
        return jnp.sum(left * right) / cells

    def apply(vector):

        def one(pair):
            field, couple = pair
            for step in range(STEPS):
                field = tangent(field, couple, advect, tables, divisor)
            return field
        stepped = lax.map(one, (vector, coupling))
        return stepped - jnp.roll(vector, -1, axis=0)
    start_norm = jnp.sqrt(inner(start_vector, start_vector))
    basis_one = start_vector / start_norm
    image_one = apply(basis_one)
    upper_one = inner(image_one, basis_one)
    residual_one = image_one - upper_one * basis_one
    lower_one = jnp.sqrt(inner(residual_one, residual_one))
    basis_two = residual_one / lower_one
    image_two = apply(basis_two)
    upper_two = inner(image_two, basis_one)
    middle_two = inner(image_two, basis_two)
    residual_two = image_two - upper_two * basis_one - middle_two * basis_two
    lower_two = jnp.sqrt(inner(residual_two, residual_two))
    next_basis = residual_two / lower_two
    hessenberg = jnp.stack([start_norm, upper_one, lower_one, upper_two, middle_two, lower_two]).astype(jnp.float32)
    return (next_basis, hessenberg)
```

```python
import functools
import math

import jax
import jax.numpy as jnp
import numpy as np
from jax import lax
from jax.experimental import pallas as pl
from jax.experimental.pallas import tpu as pltpu
from jax.sharding import PartitionSpec as P

RADIAL_ALL = 256
WINDOW_START = 124
RADIAL_GAIN = 0.25
VISC_AXIAL = 4.0
VISC_TURN = 0.05

MESH = pl.DeviceIdType.MESH
F32 = jnp.float32
BF16 = jnp.bfloat16
PARTS = 2
STRIP = 16
TILE = 256


def make_tables(count):
    index = np.arange(count)
    half = count // 2
    freq = np.where(index <= half, index, index - half)
    angle = 2.0 * np.pi / count * (freq[:, None] * index[None, :] % count)
    synth = np.where((index <= half)[:, None], np.cos(angle), np.sin(angle))
    weight = np.where((index == 0) | (index == half), 1.0 / count, 2.0 / count)
    analysis = weight[:, None] * synth
    as_bf16 = lambda table: jnp.asarray(table.astype(np.float32).astype(jnp.bfloat16))
    return as_bf16(synth), as_bf16(analysis)


def fold(value):
    total = None
    for row in range(0, value.shape[0], 8):
        for lane in range(0, value.shape[1], 128):
            piece = value[row : row + 8, lane : lane + 128]
            total = piece if total is None else total + piece
    return total


def dot(left, right):
    return jnp.dot(left, right, preferred_element_type=F32)


def steps_kernel(
    sizes, cells,
    v_hbm, couple_hbm, advect_ref, synth_k_hbm, anal_k_hbm, synth_m_hbm, anal_m_hbm,
    w1_hbm, w2_hbm, coef_ref,
    v_buf, couple, synth_k, anal_k, synth_m, anal_m,
    sent_a, sent_b, low_a, high_a, next_a, low_b, high_b, next_b,
    w1_buf, spec, mixed, inv_div, grams, slots_one, slots_two,
    load_sem, v_sem, out_sem,
    send_sem, recv_sem, sum_send, sum_recv,
):
    segs, rads, group = sizes
    chans, modes_m, modes_k = v_buf.shape
    rows = modes_m // PARTS
    pieces = [(c, q) for c in range(chans) for q in range(PARTS)]
    seg = lax.axis_index("seg")
    rad = lax.axis_index("rad")
    seg_prev = lax.rem(seg + segs - 1, segs)
    seg_next = lax.rem(seg + 1, segs)
    base = (seg // group) * group
    one_me = seg - base
    spread = segs // group
    two_count = spread * rads
    two_me = (seg // group) * rads + rad

    def one_peer(d):
        return lax.rem(one_me + d, group)

    def two_peer(d):
        other = lax.rem(two_me + d, two_count)
        return other, ((other // rads) * group + one_me, lax.rem(other, rads))

    loads = [
        pltpu.make_async_copy(source, target, load_sem.at[i])
        for i, (source, target) in enumerate(
            [
                (synth_k_hbm, synth_k),
                (synth_m_hbm, synth_m),
                (couple_hbm, couple),
                (anal_k_hbm, anal_k),
                (anal_m_hbm, anal_m),
            ]
        )
    ]
    v_loads = []
    for i, (c, q) in enumerate(pieces):
        at = (c, pl.ds(q * rows, rows))
        v_loads.append(pltpu.make_async_copy(v_hbm.at[at], v_buf.at[at], v_sem.at[i]))
        v_loads[-1].start()
    for load in loads:
        load.start()

    barrier = pltpu.get_barrier_semaphore()
    for d in range(1, group):
        pl.semaphore_signal(barrier, inc=1, device_id=(base + one_peer(d), rad), device_id_type=MESH)
    for d in range(1, two_count):
        pl.semaphore_signal(barrier, inc=1, device_id=two_peer(d)[1], device_id_type=MESH)
    for other in (seg_prev, seg_next):
        pl.semaphore_signal(barrier, inc=1, device_id=(other, rad), device_id_type=MESH)

    @pl.when(rad == 0)
    def _():
        low_a[...] = jnp.zeros_like(low_a)
        low_b[...] = jnp.zeros_like(low_b)

    @pl.when(rad == rads - 1)
    def _():
        high_a[...] = jnp.zeros_like(high_a)
        high_b[...] = jnp.zeros_like(high_b)

    def sends(phase, i):
        c, q = pieces[i]
        at = (c, pl.ds(q * rows, rows))
        source = (sent_a, sent_b)[phase]
        low, high, nxt = ((low_a, high_a, next_a), (low_b, high_b, next_b))[phase]

        def copy(way, target, device):
            return pltpu.make_async_remote_copy(
                src_ref=source.at[at], dst_ref=target.at[at],
                send_sem=send_sem.at[phase, way, i], recv_sem=recv_sem.at[phase, way, i],
                device_id=device, device_id_type=MESH,
            )

        return (
            copy(0, low, (seg, lax.rem(rad + 1, rads))),
            copy(1, high, (seg, lax.rem(rad + rads - 1, rads))),
            copy(2, nxt, (seg_prev, rad)),
        )

    def start_sends(phase, i):
        up, down, back = sends(phase, i)

        @pl.when(rad < rads - 1)
        def _():
            up.start()

        @pl.when(rad > 0)
        def _():
            down.start()

        back.start()

    def wait_recvs(phase, i):
        up, down, back = sends(phase, i)

        @pl.when(rad > 0)
        def _():
            up.wait_recv()

        @pl.when(rad < rads - 1)
        def _():
            down.wait_recv()

        back.wait_recv()

    def wait_sends(phase, i):
        up, down, back = sends(phase, i)

        @pl.when(rad < rads - 1)
        def _():
            up.wait_send()

        @pl.when(rad > 0)
        def _():
            down.wait_send()

        back.wait_send()

    def strips(c, q, body, carry):
        def step(j, carry):
            row = pl.multiple_of(q * rows + j * STRIP, STRIP)
            return body(row, pl.ds(row, STRIP), carry)

        return lax.fori_loop(0, rows // STRIP, step, carry)

    zero = jnp.zeros((8, 128), F32)
    gram = [zero] * 6
    for i, (c, q) in enumerate(pieces):
        v_loads[i].wait()

        def rounding(row, at, total, c=c):
            value = v_buf[c, at, :]
            sent_a[c, at, :] = value.astype(BF16)
            return total + fold(value * value)

        gram[0] = strips(c, q, rounding, gram[0])
        if i == 0:
            pl.semaphore_wait(barrier, group - 1 + two_count - 1 + 2)
        start_sends(0, i)

    def freq(index, count):
        return jnp.where(index <= count // 2, index, index - count // 2).astype(F32)

    freq_k = freq(lax.broadcasted_iota(jnp.int32, (1, modes_k), 1), modes_k)
    axial = VISC_AXIAL * (freq_k / (modes_k // 2)) ** 2
    wavenum = freq(lax.broadcasted_iota(jnp.int32, (1, modes_k), 1), modes_k)
    column = lax.broadcasted_iota(jnp.int32, (1, modes_k), 1)
    half = modes_k // 2
    wavenum = jnp.where(column < half, column, half - column).astype(F32)
    wavenum = wavenum * advect_ref[0]
    radius = (jnp.full((1, modes_k), rad + WINDOW_START, jnp.int32).astype(F32) + 0.5) / RADIAL_ALL

    def divide(j, _):
        row = pl.multiple_of(j * STRIP, STRIP)
        freq_m = freq(row + lax.broadcasted_iota(jnp.int32, (STRIP, modes_k), 0), modes_m)
        turning = (freq_m / (modes_m // 2)) ** 2
        inv_div[pl.ds(row, STRIP), :] = 1.0 / (1.0 + axial + VISC_TURN * turning / (radius * radius))
        return 0

    lax.fori_loop(0, modes_m // STRIP, divide, 0)

    def spectral(source):
        def synthesis(j, _):
            at = pl.ds(pl.multiple_of(j * TILE, TILE), TILE)
            physical = [
                dot(synth_m[...], dot(source[c], synth_k[:, at]).astype(BF16)) for c in range(chans)
            ]
            for c in range(chans):
                total = couple[c, 0, :, at].astype(F32) * physical[0]
                for k in range(1, chans):
                    total += couple[c, k, :, at].astype(F32) * physical[k]
                mixed[c, :, at] = total.astype(BF16)
            return 0

        lax.fori_loop(0, modes_k // TILE, synthesis, 0)

        def analysis(step, _):
            c = step // (modes_k // TILE)
            j = lax.rem(step, modes_k // TILE)
            at = pl.ds(pl.multiple_of(j * TILE, TILE), TILE)
            section = dot(mixed[c], anal_k[:, at]).astype(BF16)
            spec[c, :, at] = dot(anal_m[...], section)
            return 0

        lax.fori_loop(0, chans * (modes_k // TILE), analysis, 0)

    def image(field, bufs, c, at):
        sent, low, high, nxt = bufs
        swapped = jnp.concatenate([field[:, half:], field[:, :half]], axis=1)
        outer = low[c, at, :].astype(F32) + high[c, at, :].astype(F32)
        radial = RADIAL_GAIN * (outer - 2.0 * sent[c, at, :].astype(F32))
        total = field + spec[c, at, :] - wavenum * swapped + radial
        return total * inv_div[at, :] - nxt[c, at, :].astype(F32)

    for load in loads:
        load.wait()
    spectral(sent_a)

    w1_outs = []
    for i, (c, q) in enumerate(pieces):
        wait_recvs(0, i)

        def first(row, at, totals, c=c):
            field = v_buf[c, at, :]
            value = image(field, (sent_a, low_a, high_a, next_a), c, at)
            w1_buf[c, at, :] = value
            sent_b[c, at, :] = value.astype(BF16)
            return totals[0] + fold(value * field), totals[1] + fold(value * value)

        gram[1], gram[2] = strips(c, q, first, (gram[1], gram[2]))
        start_sends(1, i)
        at = (c, pl.ds(q * rows, rows))
        w1_outs.append(pltpu.make_async_copy(w1_buf.at[at], w1_hbm.at[at], out_sem.at[0, i]))
        w1_outs[-1].start()

    spectral(sent_b)

    w2_outs = []
    for i, (c, q) in enumerate(pieces):
        wait_recvs(1, i)

        def second(row, at, totals, c=c):
            field = w1_buf[c, at, :]
            value = image(field, (sent_b, low_b, high_b, next_b), c, at)
            spec[c, at, :] = value
            return (
                totals[0] + fold(value * v_buf[c, at, :]),
                totals[1] + fold(value * field),
                totals[2] + fold(value * value),
            )

        gram[3], gram[4], gram[5] = strips(c, q, second, (gram[3], gram[4], gram[5]))
        at = (c, pl.ds(q * rows, rows))
        w2_outs.append(pltpu.make_async_copy(spec.at[at], w2_hbm.at[at], out_sem.at[1, i]))
        w2_outs[-1].start()

    mine = jnp.concatenate([jnp.sum(value, axis=0, keepdims=True) for value in gram] + [zero[:2]], axis=0)

    def add_up(stage, slots, me, count, peer):
        def copy(d, slot):
            return pltpu.make_async_remote_copy(
                src_ref=slots.at[slot], dst_ref=slots.at[slot],
                send_sem=sum_send.at[stage, d], recv_sem=sum_recv.at[stage, d],
                device_id=peer(d), device_id_type=MESH,
            )

        for d in range(1, count):
            copy(d, me).start()
        for d in range(1, count):
            copy(d, lax.rem(me + count - d, count)).wait_recv()
        total = slots[0]
        for slot in range(1, count):
            total = total + slots[slot]
        for d in range(1, count):
            copy(d, me).wait_send()
        return total

    slots_one[one_me] = mine
    partial = add_up(0, slots_one, one_me, group, lambda d: (base + one_peer(d), rad))
    slots_two[two_me] = partial
    sums = add_up(1, slots_two, two_me, two_count, lambda d: two_peer(d)[1])
    sums = jnp.broadcast_to(jnp.sum(sums, axis=1, keepdims=True), (8, 128)) * (1.0 / cells)
    g00, g01, g11, g02, g12, g22 = (sums[i : i + 1] for i in range(6))
    start_norm = jnp.sqrt(g00)
    upper_one = g01 / g00
    lower_one = jnp.sqrt(g11 / g00 - upper_one * upper_one)
    scale = start_norm * lower_one
    upper_two = (g02 - upper_one * g01) / (g00 * lower_one)
    middle_two = (g12 - upper_one * (g02 + g11) + upper_one * upper_one * g01) / (scale * scale)
    length = (g22 - 2.0 * upper_one * g12 + upper_one * upper_one * g11) / (scale * scale)
    lower_two = jnp.sqrt(length - upper_two * upper_two - middle_two * middle_two)
    on_two = 1.0 / (scale * lower_two)
    on_one = -(upper_one + middle_two) * on_two
    on_start = (middle_two * upper_one / scale - upper_two / start_norm) / lower_two
    coef_ref[0:8, :] = jnp.concatenate(
        [start_norm, upper_one, lower_one, upper_two, middle_two, lower_two, on_two, on_one], axis=0
    )
    coef_ref[8:16, :] = jnp.broadcast_to(on_start, (8, 128))

    for i in range(len(pieces)):
        wait_sends(0, i)
        wait_sends(1, i)
        w1_outs[i].wait()
        w2_outs[i].wait()


def combine_kernel(coef_ref, v_ref, w1_ref, w2_ref, out_ref, hess_ref):
    on_two = coef_ref[6:7, 0:1]
    on_one = coef_ref[7:8, 0:1]
    on_start = coef_ref[8:9, 0:1]
    out_ref[0] = on_two * w2_ref[0] + on_one * w1_ref[0] + on_start * v_ref[0]

    @pl.when(pl.program_id(0) == 0)
    def _():
        for i in range(6):
            hess_ref[i] = coef_ref[i, 0]


def on_device(segs, rads, start_vector, coupling, advect):
    shape = start_vector.shape
    chans, modes_m, modes_k = shape[1], shape[3], shape[4]
    vector = start_vector.reshape(chans, modes_m, modes_k)
    couple = coupling.reshape(chans, chans, modes_m, modes_k)
    cells = float(segs * rads * chans * modes_m * modes_k)
    synth_m, anal_m = make_tables(modes_m)
    synth_k, anal_k = make_tables(modes_k)
    group = 16
    two_count = (segs // group) * rads
    field = (chans, modes_m, modes_k)
    count = chans * PARTS
    any_space = pl.BlockSpec(memory_space=pl.ANY)
    w1, w2, coef = pl.pallas_call(
        functools.partial(steps_kernel, (segs, rads, group), cells),
        out_shape=(
            jax.ShapeDtypeStruct(field, F32),
            jax.ShapeDtypeStruct(field, F32),
            jax.ShapeDtypeStruct((16, 128), F32),
        ),
        in_specs=[any_space, any_space, pl.BlockSpec(memory_space=pltpu.SMEM)] + [any_space] * 4,
        out_specs=(any_space, any_space, pl.BlockSpec(memory_space=pltpu.VMEM)),
        scratch_shapes=[
            pltpu.VMEM(field, F32),
            pltpu.VMEM((chans,) + field, BF16),
            pltpu.VMEM((modes_k, modes_k), BF16),
            pltpu.VMEM((modes_k, modes_k), BF16),
            pltpu.VMEM((modes_m, modes_m), BF16),
            pltpu.VMEM((modes_m, modes_m), BF16),
        ]
        + [pltpu.VMEM(field, BF16)] * 8
        + [
            pltpu.VMEM(field, F32),
            pltpu.VMEM(field, F32),
            pltpu.VMEM(field, BF16),
            pltpu.VMEM((modes_m, modes_k), F32),
            pltpu.VMEM((8, 128), F32),
            pltpu.VMEM((group, 8, 128), F32),
            pltpu.VMEM((two_count, 8, 128), F32),
            pltpu.SemaphoreType.DMA((5,)),
            pltpu.SemaphoreType.DMA((count,)),
            pltpu.SemaphoreType.DMA((2, count)),
            pltpu.SemaphoreType.DMA((2, 3, count)),
            pltpu.SemaphoreType.DMA((2, 3, count)),
            pltpu.SemaphoreType.DMA((2, 16)),
            pltpu.SemaphoreType.DMA((2, 16)),
        ],
        compiler_params=pltpu.CompilerParams(
            collective_id=0, has_side_effects=True, vmem_limit_bytes=50 * 1024 * 1024
        ),
    )(vector, couple, advect, synth_k, anal_k.T, synth_m.T, anal_m)
    block = (1, modes_m // 2, modes_k)
    block_spec = pl.BlockSpec(block, lambda c, q: (c, q, 0))
    out, hess = pl.pallas_call(
        combine_kernel,
        grid=(chans, 2),
        out_shape=(jax.ShapeDtypeStruct(field, F32), jax.ShapeDtypeStruct((6,), F32)),
        in_specs=[pl.BlockSpec((16, 128), lambda c, q: (0, 0))] + [block_spec] * 3,
        out_specs=(block_spec, pl.BlockSpec(memory_space=pltpu.SMEM)),
    )(coef, vector, w1, w2)
    return out.reshape(shape), hess


def solution(mesh):
    return jax.shard_map(
        functools.partial(on_device, mesh.shape["seg"], mesh.shape["rad"]),
        mesh=mesh,
        in_specs=(
            P("seg", None, "rad", None, None),
            P("seg", None, None, "rad", None, None),
            P("rad"),
        ),
        out_specs=(P("seg", None, "rad", None, None), P()),
        check_vma=False,
    )
```

```python
import functools
import math

import jax
import jax.numpy as jnp
import numpy as np
from jax import lax
from jax.experimental import pallas as pl
from jax.experimental.pallas import tpu as pltpu
from jax.sharding import PartitionSpec as P

RADIAL_ALL = 256
WINDOW_START = 124
RADIAL_GAIN = 0.25
VISC_AXIAL = 4.0
VISC_TURN = 0.05

MESH = pl.DeviceIdType.MESH
F32 = jnp.float32
BF16 = jnp.bfloat16
PARTS = 2
STRIP = 16
TILE = 256
LINE = 4
OUT_ROWS = 96
VMEM_LIMIT = 34 * 1024 * 1024


def make_tables(count):
    index = np.arange(count)
    half = count // 2
    freq = np.where(index <= half, index, index - half)
    angle = 2.0 * np.pi / count * (freq[:, None] * index[None, :] % count)
    synth = np.where((index <= half)[:, None], np.cos(angle), np.sin(angle))
    weight = np.where((index == 0) | (index == half), 1.0 / count, 2.0 / count)
    analysis = weight[:, None] * synth
    as_bf16 = lambda table: jnp.asarray(table.astype(np.float32).astype(jnp.bfloat16))
    return as_bf16(synth), as_bf16(analysis)


def fold(value):
    total = None
    for row in range(0, value.shape[0], 8):
        for lane in range(0, value.shape[1], 128):
            piece = value[row : row + 8, lane : lane + 128]
            total = piece if total is None else total + piece
    return total


def dot(left, right):
    return jnp.dot(left, right, preferred_element_type=F32)


def steps_kernel(
    sizes, cells,
    v_hbm, couple_hbm, advect_ref, synth_k_hbm, anal_k_hbm, synth_m_hbm, anal_m_hbm,
    v_buf, w1_buf, spec, coef_ref,
    couple, synth_k, anal_k, synth_m, anal_m,
    sent_a, sent_b, low_a, high_a, next_a, low_b, high_b, next_b,
    relay_a, relay_b, mixed, inv_div, grams, slots_one, slots_two,
    load_sem, v_sem,
    send_sem, recv_sem, hop_send, hop_recv, sum_send, sum_recv,
):
    segs, rads, group = sizes
    chans, modes_m, modes_k = v_buf.shape
    rows = modes_m // PARTS
    pieces = [(c, q) for c in range(chans) for q in range(PARTS)]
    seg = lax.axis_index("seg")
    rad = lax.axis_index("rad")
    seg_prev = lax.rem(seg + segs - 1, segs)
    seg_next = lax.rem(seg + 1, segs)
    base = (seg // group) * group
    one_me = seg - base
    spread = segs // group
    two_count = spread * rads
    two_me = (seg // group) * rads + rad

    def one_peer(d):
        return lax.rem(one_me + d, group)

    def two_peer(d):
        other = lax.rem(two_me + d, two_count)
        return other, ((other // rads) * group + one_me, lax.rem(other, rads))

    upper_half = seg // group
    column, line = rad // LINE, lax.rem(rad, LINE)
    at_edge = ((upper_half == 0) & (line == 0)) | ((upper_half == 1) & (line == LINE - 1))
    at_far = ((upper_half == 1) & (line == 0)) | ((upper_half == 0) & (line == LINE - 1))
    is_source = (one_me == 0) & at_edge
    is_sink = (one_me == group - 1) & at_far
    is_relay = (one_me == 1) & ((line == 0) | (line == LINE - 1)) & (upper_half == column)
    relay = ((1 - column) * group + 1, (1 - column) * LINE + line)
    relayed_rad = (1 - column) * LINE + line
    relayed_source = (jnp.where(line == 0, 0, group), relayed_rad)
    relayed_sink = (jnp.where(line == 0, segs - 1, group - 1), relayed_rad)

    loads = [
        pltpu.make_async_copy(source, target, load_sem.at[i])
        for i, (source, target) in enumerate(
            [
                (synth_k_hbm, synth_k),
                (synth_m_hbm, synth_m),
                (couple_hbm, couple),
                (anal_k_hbm, anal_k),
                (anal_m_hbm, anal_m),
            ]
        )
    ]
    v_loads = []
    for i, (c, q) in enumerate(pieces):
        at = (c, pl.ds(q * rows, rows))
        v_loads.append(pltpu.make_async_copy(v_hbm.at[at], v_buf.at[at], v_sem.at[i]))
        v_loads[-1].start()
    for load in loads:
        load.start()

    barrier = pltpu.get_barrier_semaphore()
    for d in range(1, group):
        pl.semaphore_signal(barrier, inc=1, device_id=(base + one_peer(d), rad), device_id_type=MESH)
    for d in range(1, two_count):
        pl.semaphore_signal(barrier, inc=1, device_id=two_peer(d)[1], device_id_type=MESH)
    for other in (seg_prev, seg_next):
        pl.semaphore_signal(barrier, inc=1, device_id=(other, rad), device_id_type=MESH)

    def signal(device):
        pl.semaphore_signal(barrier, inc=1, device_id=device, device_id_type=MESH)

    @pl.when(is_source | is_sink)
    def _():
        signal(relay)

    @pl.when(is_relay)
    def _():
        signal(relayed_source)
        signal(relayed_sink)

    @pl.when(rad == 0)
    def _():
        low_a[...] = jnp.zeros_like(low_a)
        low_b[...] = jnp.zeros_like(low_b)

    @pl.when(rad == rads - 1)
    def _():
        high_a[...] = jnp.zeros_like(high_a)
        high_b[...] = jnp.zeros_like(high_b)

    def sends(phase, i):
        c, q = pieces[i]
        at = (c, pl.ds(q * rows, rows))
        source = (sent_a, sent_b)[phase]
        low, high, nxt = ((low_a, high_a, next_a), (low_b, high_b, next_b))[phase]

        def copy(way, target, device):
            return pltpu.make_async_remote_copy(
                src_ref=source.at[at], dst_ref=target.at[at],
                send_sem=send_sem.at[phase, way, i], recv_sem=recv_sem.at[phase, way, i],
                device_id=device, device_id_type=MESH,
            )

        return (
            copy(0, low, (seg, lax.rem(rad + 1, rads))),
            copy(1, high, (seg, lax.rem(rad + rads - 1, rads))),
            copy(2, nxt, (seg_prev, rad)),
        )

    def hop(phase, i):
        c, q = pieces[i]
        at = (c, pl.ds(q * rows, rows))
        return pltpu.make_async_remote_copy(
            src_ref=(sent_a, sent_b)[phase].at[at], dst_ref=(relay_a, relay_b)[phase].at[at],
            send_sem=hop_send.at[phase, 0, i], recv_sem=hop_recv.at[phase, i],
            device_id=relay, device_id_type=MESH,
        )

    def onward(phase, i):
        c, q = pieces[i]
        at = (c, pl.ds(q * rows, rows))
        return pltpu.make_async_remote_copy(
            src_ref=(relay_a, relay_b)[phase].at[at], dst_ref=(next_a, next_b)[phase].at[at],
            send_sem=hop_send.at[phase, 1, i], recv_sem=recv_sem.at[phase, 2, i],
            device_id=relayed_sink, device_id_type=MESH,
        )

    def pass_on(phase, i):
        @pl.when(is_relay)
        def _():
            for j in ([0] if i == 0 else []) + ([i + 1] if i + 1 < len(pieces) else []):
                hop(phase, j).wait_recv()
                onward(phase, j).start()

    def start_sends(phase, i):
        up, down, back = sends(phase, i)

        @pl.when(rad < rads - 1)
        def _():
            up.start()

        @pl.when(rad > 0)
        def _():
            down.start()

        @pl.when(is_source)
        def _():
            hop(phase, i).start()

        @pl.when(jnp.logical_not(is_source))
        def _():
            back.start()

    def wait_recvs(phase, i):
        up, down, back = sends(phase, i)

        @pl.when(rad > 0)
        def _():
            up.wait_recv()

        @pl.when(rad < rads - 1)
        def _():
            down.wait_recv()

        back.wait_recv()

    def wait_sends(phase, i):
        up, down, back = sends(phase, i)

        @pl.when(rad < rads - 1)
        def _():
            up.wait_send()

        @pl.when(rad > 0)
        def _():
            down.wait_send()

        @pl.when(is_source)
        def _():
            hop(phase, i).wait_send()

        @pl.when(jnp.logical_not(is_source))
        def _():
            back.wait_send()

        @pl.when(is_relay)
        def _():
            onward(phase, i).wait_send()

    def strips(c, q, body, carry):
        def step(j, carry):
            row = pl.multiple_of(q * rows + j * STRIP, STRIP)
            return body(row, pl.ds(row, STRIP), carry)

        return lax.fori_loop(0, rows // STRIP, step, carry)

    zero = jnp.zeros((8, 128), F32)
    gram = [zero] * 6
    for i, (c, q) in enumerate(pieces):
        v_loads[i].wait()

        def rounding(row, at, total, c=c):
            value = v_buf[c, at, :]
            sent_a[c, at, :] = value.astype(BF16)
            return total + fold(value * value)

        gram[0] = strips(c, q, rounding, gram[0])
        if i == 0:
            extra = jnp.where(is_relay, 2, jnp.where(is_source | is_sink, 1, 0))
            pl.semaphore_wait(barrier, group - 1 + two_count - 1 + 2 + extra)
        start_sends(0, i)

    def freq(index, count):
        return jnp.where(index <= count // 2, index, index - count // 2).astype(F32)

    freq_k = freq(lax.broadcasted_iota(jnp.int32, (1, modes_k), 1), modes_k)
    axial = VISC_AXIAL * (freq_k / (modes_k // 2)) ** 2
    mode = lax.broadcasted_iota(jnp.int32, (1, modes_k), 1)
    half = modes_k // 2
    wavenum = jnp.where(mode < half, mode, half - mode).astype(F32) * advect_ref[0]
    radius = (jnp.full((1, modes_k), rad + WINDOW_START, jnp.int32).astype(F32) + 0.5) / RADIAL_ALL

    def divide(j, _):
        row = pl.multiple_of(j * STRIP, STRIP)
        freq_m = freq(row + lax.broadcasted_iota(jnp.int32, (STRIP, modes_k), 0), modes_m)
        turning = (freq_m / (modes_m // 2)) ** 2
        inv_div[pl.ds(row, STRIP), :] = 1.0 / (1.0 + axial + VISC_TURN * turning / (radius * radius))
        return 0

    lax.fori_loop(0, modes_m // STRIP, divide, 0)

    def spectral(source):
        def synthesis(j, _):
            at = pl.ds(pl.multiple_of(j * TILE, TILE), TILE)
            physical = [
                dot(synth_m[...], dot(source[c], synth_k[:, at]).astype(BF16)) for c in range(chans)
            ]
            for c in range(chans):
                total = couple[c, 0, :, at].astype(F32) * physical[0]
                for k in range(1, chans):
                    total += couple[c, k, :, at].astype(F32) * physical[k]
                mixed[c, :, at] = total.astype(BF16)
            return 0

        lax.fori_loop(0, modes_k // TILE, synthesis, 0)

        def analysis(step, _):
            c = step // (modes_k // TILE)
            j = lax.rem(step, modes_k // TILE)
            at = pl.ds(pl.multiple_of(j * TILE, TILE), TILE)
            section = dot(mixed[c], anal_k[:, at]).astype(BF16)
            spec[c, :, at] = dot(anal_m[...], section)
            return 0

        lax.fori_loop(0, chans * (modes_k // TILE), analysis, 0)

    def image(field, bufs, c, at):
        sent, low, high, nxt = bufs
        swapped = jnp.concatenate([field[:, half:], field[:, :half]], axis=1)
        outer = low[c, at, :].astype(F32) + high[c, at, :].astype(F32)
        radial = RADIAL_GAIN * (outer - 2.0 * sent[c, at, :].astype(F32))
        total = field + spec[c, at, :] - wavenum * swapped + radial
        return total * inv_div[at, :] - nxt[c, at, :].astype(F32)

    for load in loads:
        load.wait()
    spectral(sent_a)

    for i, (c, q) in enumerate(pieces):
        pass_on(0, i)
        wait_recvs(0, i)

        def first(row, at, totals, c=c):
            field = v_buf[c, at, :]
            value = image(field, (sent_a, low_a, high_a, next_a), c, at)
            w1_buf[c, at, :] = value
            sent_b[c, at, :] = value.astype(BF16)
            return totals[0] + fold(value * field), totals[1] + fold(value * value)

        gram[1], gram[2] = strips(c, q, first, (gram[1], gram[2]))
        start_sends(1, i)

    spectral(sent_b)

    for i, (c, q) in enumerate(pieces):
        pass_on(1, i)
        wait_recvs(1, i)

        def second(row, at, totals, c=c):
            field = w1_buf[c, at, :]
            value = image(field, (sent_b, low_b, high_b, next_b), c, at)
            spec[c, at, :] = value
            return (
                totals[0] + fold(value * v_buf[c, at, :]),
                totals[1] + fold(value * field),
                totals[2] + fold(value * value),
            )

        gram[3], gram[4], gram[5] = strips(c, q, second, (gram[3], gram[4], gram[5]))

    mine = jnp.concatenate([jnp.sum(value, axis=0, keepdims=True) for value in gram] + [zero[:2]], axis=0)

    def add_up(stage, slots, me, count, peer):
        def copy(d, slot):
            return pltpu.make_async_remote_copy(
                src_ref=slots.at[slot], dst_ref=slots.at[slot],
                send_sem=sum_send.at[stage, d], recv_sem=sum_recv.at[stage, d],
                device_id=peer(d), device_id_type=MESH,
            )

        for d in range(1, count):
            copy(d, me).start()
        for d in range(1, count):
            copy(d, lax.rem(me + count - d, count)).wait_recv()
        total = slots[0]
        for slot in range(1, count):
            total = total + slots[slot]
        for d in range(1, count):
            copy(d, me).wait_send()
        return total

    slots_one[one_me] = mine
    partial = add_up(0, slots_one, one_me, group, lambda d: (base + one_peer(d), rad))
    slots_two[two_me] = partial
    sums = add_up(1, slots_two, two_me, two_count, lambda d: two_peer(d)[1])
    sums = jnp.broadcast_to(jnp.sum(sums, axis=1, keepdims=True), (8, 128)) * (1.0 / cells)
    g00, g01, g11, g02, g12, g22 = (sums[i : i + 1] for i in range(6))
    start_norm = jnp.sqrt(g00)
    upper_one = g01 / g00
    lower_one = jnp.sqrt(g11 / g00 - upper_one * upper_one)
    scale = start_norm * lower_one
    upper_two = (g02 - upper_one * g01) / (g00 * lower_one)
    middle_two = (g12 - upper_one * (g02 + g11) + upper_one * upper_one * g01) / (scale * scale)
    length = (g22 - 2.0 * upper_one * g12 + upper_one * upper_one * g11) / (scale * scale)
    lower_two = jnp.sqrt(length - upper_two * upper_two - middle_two * middle_two)
    on_two = 1.0 / (scale * lower_two)
    on_one = -(upper_one + middle_two) * on_two
    on_start = (middle_two * upper_one / scale - upper_two / start_norm) / lower_two
    coef_ref[0:8, :] = jnp.concatenate(
        [start_norm, upper_one, lower_one, upper_two, middle_two, lower_two, on_two, on_one], axis=0
    )
    coef_ref[8:16, :] = jnp.broadcast_to(on_start, (8, 128))

    for i in range(len(pieces)):
        wait_sends(0, i)
        wait_sends(1, i)


def combine_kernel(coef_ref, v_ref, w1_ref, w2_ref, out_ref, hess_ref, stage, sem):
    chans, modes_m, modes_k = v_ref.shape
    on_two = jnp.broadcast_to(coef_ref[6:7, 0:1], (8, modes_k))
    on_one = jnp.broadcast_to(coef_ref[7:8, 0:1], (8, modes_k))
    on_start = jnp.broadcast_to(coef_ref[8:9, 0:1], (8, modes_k))
    pieces = [(c, row) for c in range(chans) for row in range(0, modes_m, OUT_ROWS)]

    def copy(i):
        c, row = pieces[i]
        return pltpu.make_async_copy(
            stage.at[i % 2], out_ref.at[c, pl.ds(row, OUT_ROWS)], sem.at[i % 2]
        )

    for i, (c, row) in enumerate(pieces):
        if i >= 2:
            copy(i - 2).wait()

        def strip(j, _, i=i, c=c, row=row):
            at = pl.ds(pl.multiple_of(row + j * 8, 8), 8)
            to = pl.ds(pl.multiple_of(j * 8, 8), 8)
            stage[i % 2, to, :] = (
                on_two * w2_ref[c, at, :] + on_one * w1_ref[c, at, :] + on_start * v_ref[c, at, :]
            )
            return 0

        lax.fori_loop(0, OUT_ROWS // 8, strip, 0)
        copy(i).start()
    for i in range(6):
        hess_ref[i] = coef_ref[i, 0]
    copy(len(pieces) - 2).wait()
    copy(len(pieces) - 1).wait()


def on_device(segs, rads, start_vector, coupling, advect):
    shape = start_vector.shape
    chans, modes_m, modes_k = shape[1], shape[3], shape[4]
    vector = start_vector.reshape(chans, modes_m, modes_k)
    couple = coupling.reshape(chans, chans, modes_m, modes_k)
    cells = float(segs * rads * chans * modes_m * modes_k)
    synth_m, anal_m = make_tables(modes_m)
    synth_k, anal_k = make_tables(modes_k)
    group = 16
    two_count = (segs // group) * rads
    field = (chans, modes_m, modes_k)
    count = chans * PARTS
    in_place = lambda value: pltpu.with_memory_space_constraint(value, pltpu.HBM)
    tables = (synth_k, anal_k.T, synth_m.T, anal_m)
    in_hbm = pl.BlockSpec(memory_space=pltpu.HBM)
    in_vmem = pl.BlockSpec(memory_space=pltpu.VMEM)
    v, w1, w2, coef = pl.pallas_call(
        functools.partial(steps_kernel, (segs, rads, group), cells),
        out_shape=[jax.ShapeDtypeStruct(field, F32)] * 3 + [jax.ShapeDtypeStruct((16, 128), F32)],
        in_specs=[in_hbm, in_hbm, pl.BlockSpec(memory_space=pltpu.SMEM)] + [in_hbm] * 4,
        out_specs=[in_vmem] * 4,
        scratch_shapes=[
            pltpu.VMEM((chans,) + field, BF16),
            pltpu.VMEM((modes_k, modes_k), BF16),
            pltpu.VMEM((modes_k, modes_k), BF16),
            pltpu.VMEM((modes_m, modes_m), BF16),
            pltpu.VMEM((modes_m, modes_m), BF16),
        ]
        + [pltpu.VMEM(field, BF16)] * 11
        + [
            pltpu.VMEM((modes_m, modes_k), F32),
            pltpu.VMEM((8, 128), F32),
            pltpu.VMEM((group, 8, 128), F32),
            pltpu.VMEM((two_count, 8, 128), F32),
            pltpu.SemaphoreType.DMA((5,)),
            pltpu.SemaphoreType.DMA((count,)),
            pltpu.SemaphoreType.DMA((2, 3, count)),
            pltpu.SemaphoreType.DMA((2, 3, count)),
            pltpu.SemaphoreType.DMA((2, 2, count)),
            pltpu.SemaphoreType.DMA((2, count)),
            pltpu.SemaphoreType.DMA((2, 16)),
            pltpu.SemaphoreType.DMA((2, 16)),
        ],
        compiler_params=pltpu.CompilerParams(
            collective_id=0, has_side_effects=True, vmem_limit_bytes=VMEM_LIMIT
        ),
    )(in_place(vector), in_place(couple), advect, *map(in_place, tables))
    out, hess = pl.pallas_call(
        combine_kernel,
        out_shape=(jax.ShapeDtypeStruct(field, F32), jax.ShapeDtypeStruct((6,), F32)),
        in_specs=[in_vmem] * 4,
        out_specs=(in_hbm, pl.BlockSpec(memory_space=pltpu.SMEM)),
        scratch_shapes=[
            pltpu.VMEM((2, OUT_ROWS, modes_k), F32),
            pltpu.SemaphoreType.DMA((2,)),
        ],
        compiler_params=pltpu.CompilerParams(vmem_limit_bytes=VMEM_LIMIT),
    )(coef, v, w1, w2)
    return out.reshape(shape), hess


def solution(mesh):
    return jax.shard_map(
        functools.partial(on_device, mesh.shape["seg"], mesh.shape["rad"]),
        mesh=mesh,
        in_specs=(
            P("seg", None, "rad", None, None),
            P("seg", None, None, "rad", None, None),
            P("rad"),
        ),
        out_specs=(P("seg", None, "rad", None, None), P()),
        check_vma=False,
    )
```

```python
import functools
import math

import jax
import jax.numpy as jnp
import numpy as np
from jax import lax
from jax.experimental import pallas as pl
from jax.experimental.pallas import tpu as pltpu
from jax.sharding import PartitionSpec as P

RADIAL_ALL = 256
WINDOW_START = 124
RADIAL_GAIN = 0.25
VISC_AXIAL = 4.0
VISC_TURN = 0.05

MESH = pl.DeviceIdType.MESH
F32 = jnp.float32
BF16 = jnp.bfloat16
PARTS = 2
STRIP = 16
TILE = 256
LINE = 4
OUT_ROWS = 96
OUT_STRIP = 32
VMEM_LIMIT = 34 * 1024 * 1024


def make_tables(count):
    index = np.arange(count)
    half = count // 2
    freq = np.where(index <= half, index, index - half)
    angle = 2.0 * np.pi / count * (freq[:, None] * index[None, :] % count)
    synth = np.where((index <= half)[:, None], np.cos(angle), np.sin(angle))
    weight = np.where((index == 0) | (index == half), 1.0 / count, 2.0 / count)
    analysis = weight[:, None] * synth
    as_bf16 = lambda table: jnp.asarray(table.astype(np.float32).astype(jnp.bfloat16))
    return as_bf16(synth), as_bf16(analysis)


def fold(value):
    total = None
    for row in range(0, value.shape[0], 8):
        for lane in range(0, value.shape[1], 128):
            piece = value[row : row + 8, lane : lane + 128]
            total = piece if total is None else total + piece
    return total


def dot(left, right):
    return jnp.dot(left, right, preferred_element_type=F32)


def steps_kernel(
    sizes, cells,
    v_hbm, couple_hbm, advect_ref, synth_k_hbm, anal_k_hbm, synth_m_hbm, anal_m_hbm,
    v_buf, w1_buf, spec, coef_ref,
    couple, synth_k, anal_k, synth_m, anal_m,
    sent_a, sent_b, low_a, high_a, next_a, low_b, high_b, next_b,
    relay_a, relay_b, mixed, inv_div, grams, slots_one, slots_two,
    load_sem, v_sem,
    send_sem, recv_sem, hop_send, hop_recv, sum_send, sum_recv,
):
    segs, rads, group = sizes
    chans, modes_m, modes_k = v_buf.shape
    rows = modes_m // PARTS
    pieces = [(c, q) for c in range(chans) for q in range(PARTS)]
    seg = lax.axis_index("seg")
    rad = lax.axis_index("rad")
    seg_prev = lax.rem(seg + segs - 1, segs)
    seg_next = lax.rem(seg + 1, segs)
    base = (seg // group) * group
    one_me = seg - base
    spread = segs // group
    two_count = spread * rads
    two_me = (seg // group) * rads + rad

    def one_peer(d):
        return lax.rem(one_me + d, group)

    def two_peer(d):
        other = lax.rem(two_me + d, two_count)
        return other, ((other // rads) * group + one_me, lax.rem(other, rads))

    upper_half = seg // group
    column, line = rad // LINE, lax.rem(rad, LINE)
    far_rad = (1 - column) * LINE + line
    detoured = ((line == LINE - 1) & (column == 0)) | ((line == 0) & (column == 1))
    is_source = (one_me == 0) & detoured
    is_sink = (one_me == group - 1) & detoured
    is_relay = (one_me == 1) & (((line == LINE - 1) & (column == 1)) | ((line == 0) & (column == 0)))
    relay = ((1 - upper_half) * group + 1, far_rad)
    relayed_source = ((1 - upper_half) * group, far_rad)
    relayed_sink = (base + group - 1, far_rad)

    loads = [
        pltpu.make_async_copy(source, target, load_sem.at[i])
        for i, (source, target) in enumerate(
            [
                (synth_k_hbm, synth_k),
                (synth_m_hbm, synth_m),
                (couple_hbm, couple),
                (anal_k_hbm, anal_k),
                (anal_m_hbm, anal_m),
            ]
        )
    ]
    v_loads = []
    for i, (c, q) in enumerate(pieces):
        at = (c, pl.ds(q * rows, rows))
        v_loads.append(pltpu.make_async_copy(v_hbm.at[at], v_buf.at[at], v_sem.at[i]))
        v_loads[-1].start()
    for load in loads:
        load.start()

    barrier = pltpu.get_barrier_semaphore()
    for d in range(1, group):
        pl.semaphore_signal(barrier, inc=1, device_id=(base + one_peer(d), rad), device_id_type=MESH)
    for d in range(1, two_count):
        pl.semaphore_signal(barrier, inc=1, device_id=two_peer(d)[1], device_id_type=MESH)
    for other in (seg_prev, seg_next):
        pl.semaphore_signal(barrier, inc=1, device_id=(other, rad), device_id_type=MESH)

    def signal(device):
        pl.semaphore_signal(barrier, inc=1, device_id=device, device_id_type=MESH)

    @pl.when(is_source)
    def _():
        signal(relay)

    @pl.when(is_sink)
    def _():
        signal((base + 1, far_rad))

    @pl.when(is_relay)
    def _():
        signal(relayed_source)
        signal(relayed_sink)

    def sends(phase, i):
        c, q = pieces[i]
        at = (c, pl.ds(q * rows, rows))
        source = (sent_a, sent_b)[phase]
        low, high, nxt = ((low_a, high_a, next_a), (low_b, high_b, next_b))[phase]

        def copy(way, target, device):
            return pltpu.make_async_remote_copy(
                src_ref=source.at[at], dst_ref=target.at[at],
                send_sem=send_sem.at[phase, way, i], recv_sem=recv_sem.at[phase, way, i],
                device_id=device, device_id_type=MESH,
            )

        return (
            copy(0, low, (seg, lax.rem(rad + 1, rads))),
            copy(1, high, (seg, lax.rem(rad + rads - 1, rads))),
            copy(2, nxt, (seg_prev, rad)),
        )

    def hop(phase, i):
        c, q = pieces[i]
        at = (c, pl.ds(q * rows, rows))
        return pltpu.make_async_remote_copy(
            src_ref=(sent_a, sent_b)[phase].at[at], dst_ref=(relay_a, relay_b)[phase].at[at],
            send_sem=hop_send.at[phase, 0, i], recv_sem=hop_recv.at[phase, i],
            device_id=relay, device_id_type=MESH,
        )

    def onward(phase, i):
        c, q = pieces[i]
        at = (c, pl.ds(q * rows, rows))
        return pltpu.make_async_remote_copy(
            src_ref=(relay_a, relay_b)[phase].at[at], dst_ref=(next_a, next_b)[phase].at[at],
            send_sem=hop_send.at[phase, 1, i], recv_sem=recv_sem.at[phase, 2, i],
            device_id=relayed_sink, device_id_type=MESH,
        )

    def pass_on(phase, i):
        @pl.when(is_relay)
        def _():
            for j in ([0] if i == 0 else []) + ([i + 1] if i + 1 < len(pieces) else []):
                hop(phase, j).wait_recv()
                onward(phase, j).start()

    def start_sends(phase, i):
        up, down, back = sends(phase, i)

        @pl.when(rad < rads - 1)
        def _():
            up.start()

        @pl.when(rad > 0)
        def _():
            down.start()

        @pl.when(is_source)
        def _():
            hop(phase, i).start()

        @pl.when(jnp.logical_not(is_source))
        def _():
            back.start()

    def wait_recvs(phase, i):
        up, down, back = sends(phase, i)

        @pl.when(rad > 0)
        def _():
            up.wait_recv()

        @pl.when(rad < rads - 1)
        def _():
            down.wait_recv()

        back.wait_recv()

    def wait_sends(phase, i):
        up, down, back = sends(phase, i)

        @pl.when(rad < rads - 1)
        def _():
            up.wait_send()

        @pl.when(rad > 0)
        def _():
            down.wait_send()

        @pl.when(is_source)
        def _():
            hop(phase, i).wait_send()

        @pl.when(jnp.logical_not(is_source))
        def _():
            back.wait_send()

        @pl.when(is_relay)
        def _():
            onward(phase, i).wait_send()

    def strips(c, q, body, carry):
        def step(j, carry):
            row = pl.multiple_of(q * rows + j * STRIP, STRIP)
            return body(row, pl.ds(row, STRIP), carry)

        return lax.fori_loop(0, rows // STRIP, step, carry)

    zero = jnp.zeros((8, 128), F32)
    gram = [zero] * 6
    for i, (c, q) in enumerate(pieces):
        v_loads[i].wait()

        def rounding(row, at, total, c=c):
            value = v_buf[c, at, :]
            sent_a[c, at, :] = value.astype(BF16)
            return total + fold(value * value)

        gram[0] = strips(c, q, rounding, gram[0])
        if i == 0:
            extra = jnp.where(is_relay, 2, jnp.where(is_source | is_sink, 1, 0))
            pl.semaphore_wait(barrier, group - 1 + two_count - 1 + 2 + extra)
        start_sends(0, i)

    @pl.when(rad == 0)
    def _():
        low_a[...] = jnp.zeros_like(low_a)
        low_b[...] = jnp.zeros_like(low_b)

    @pl.when(rad == rads - 1)
    def _():
        high_a[...] = jnp.zeros_like(high_a)
        high_b[...] = jnp.zeros_like(high_b)

    def freq(index, count):
        return jnp.where(index <= count // 2, index, index - count // 2).astype(F32)

    freq_k = freq(lax.broadcasted_iota(jnp.int32, (1, modes_k), 1), modes_k)
    axial = VISC_AXIAL * (freq_k / (modes_k // 2)) ** 2
    mode = lax.broadcasted_iota(jnp.int32, (1, modes_k), 1)
    half = modes_k // 2
    wavenum = jnp.where(mode < half, mode, half - mode).astype(F32) * advect_ref[0]
    radius = (jnp.full((1, modes_k), rad + WINDOW_START, jnp.int32).astype(F32) + 0.5) / RADIAL_ALL

    def divide(j, _):
        row = pl.multiple_of(j * STRIP, STRIP)
        freq_m = freq(row + lax.broadcasted_iota(jnp.int32, (STRIP, modes_k), 0), modes_m)
        turning = (freq_m / (modes_m // 2)) ** 2
        inv_div[pl.ds(row, STRIP), :] = 1.0 / (1.0 + axial + VISC_TURN * turning / (radius * radius))
        return 0

    lax.fori_loop(0, modes_m // STRIP, divide, 0)

    def spectral(source):
        def synthesis(j, _):
            at = pl.ds(pl.multiple_of(j * TILE, TILE), TILE)
            physical = [
                dot(synth_m[...], dot(source[c], synth_k[:, at]).astype(BF16)) for c in range(chans)
            ]
            for c in range(chans):
                total = couple[c, 0, :, at].astype(F32) * physical[0]
                for k in range(1, chans):
                    total += couple[c, k, :, at].astype(F32) * physical[k]
                mixed[c, :, at] = total.astype(BF16)
            return 0

        lax.fori_loop(0, modes_k // TILE, synthesis, 0)

        def analysis(step, _):
            c = step // (modes_k // TILE)
            j = lax.rem(step, modes_k // TILE)
            at = pl.ds(pl.multiple_of(j * TILE, TILE), TILE)
            section = dot(mixed[c], anal_k[:, at]).astype(BF16)
            spec[c, :, at] = dot(anal_m[...], section)
            return 0

        lax.fori_loop(0, chans * (modes_k // TILE), analysis, 0)

    def image(field, bufs, c, at):
        sent, low, high, nxt = bufs
        swapped = jnp.concatenate([field[:, half:], field[:, :half]], axis=1)
        outer = low[c, at, :].astype(F32) + high[c, at, :].astype(F32)
        radial = RADIAL_GAIN * (outer - 2.0 * sent[c, at, :].astype(F32))
        total = field + spec[c, at, :] - wavenum * swapped + radial
        return total * inv_div[at, :] - nxt[c, at, :].astype(F32)

    for load in loads:
        load.wait()
    spectral(sent_a)

    for i, (c, q) in enumerate(pieces):
        pass_on(0, i)
        wait_recvs(0, i)

        def first(row, at, totals, c=c):
            field = v_buf[c, at, :]
            value = image(field, (sent_a, low_a, high_a, next_a), c, at)
            w1_buf[c, at, :] = value
            sent_b[c, at, :] = value.astype(BF16)
            return totals[0] + fold(value * field), totals[1] + fold(value * value)

        gram[1], gram[2] = strips(c, q, first, (gram[1], gram[2]))
        start_sends(1, i)

    spectral(sent_b)

    for i, (c, q) in enumerate(pieces):
        pass_on(1, i)
        wait_recvs(1, i)

        def second(row, at, totals, c=c):
            field = w1_buf[c, at, :]
            value = image(field, (sent_b, low_b, high_b, next_b), c, at)
            spec[c, at, :] = value
            return (
                totals[0] + fold(value * v_buf[c, at, :]),
                totals[1] + fold(value * field),
                totals[2] + fold(value * value),
            )

        gram[3], gram[4], gram[5] = strips(c, q, second, (gram[3], gram[4], gram[5]))

    mine = jnp.concatenate([jnp.sum(value, axis=0, keepdims=True) for value in gram] + [zero[:2]], axis=0)

    def add_up(stage, slots, me, count, peer):
        def copy(d, slot):
            return pltpu.make_async_remote_copy(
                src_ref=slots.at[slot], dst_ref=slots.at[slot],
                send_sem=sum_send.at[stage, d], recv_sem=sum_recv.at[stage, d],
                device_id=peer(d), device_id_type=MESH,
            )

        for d in range(1, count):
            copy(d, me).start()
        for d in range(1, count):
            copy(d, lax.rem(me + count - d, count)).wait_recv()
        total = slots[0]
        for slot in range(1, count):
            total = total + slots[slot]
        for d in range(1, count):
            copy(d, me).wait_send()
        return total

    slots_one[one_me] = mine
    partial = add_up(0, slots_one, one_me, group, lambda d: (base + one_peer(d), rad))
    slots_two[two_me] = partial
    sums = add_up(1, slots_two, two_me, two_count, lambda d: two_peer(d)[1])
    sums = jnp.broadcast_to(jnp.sum(sums, axis=1, keepdims=True), (8, 128)) * (1.0 / cells)
    g00, g01, g11, g02, g12, g22 = (sums[i : i + 1] for i in range(6))
    start_norm = jnp.sqrt(g00)
    upper_one = g01 / g00
    lower_one = jnp.sqrt(g11 / g00 - upper_one * upper_one)
    scale = start_norm * lower_one
    upper_two = (g02 - upper_one * g01) / (g00 * lower_one)
    middle_two = (g12 - upper_one * (g02 + g11) + upper_one * upper_one * g01) / (scale * scale)
    length = (g22 - 2.0 * upper_one * g12 + upper_one * upper_one * g11) / (scale * scale)
    lower_two = jnp.sqrt(length - upper_two * upper_two - middle_two * middle_two)
    on_two = 1.0 / (scale * lower_two)
    on_one = -(upper_one + middle_two) * on_two
    on_start = (middle_two * upper_one / scale - upper_two / start_norm) / lower_two
    coef_ref[0:8, :] = jnp.concatenate(
        [start_norm, upper_one, lower_one, upper_two, middle_two, lower_two, on_two, on_one], axis=0
    )
    coef_ref[8:16, :] = jnp.broadcast_to(on_start, (8, 128))

    for i in range(len(pieces)):
        wait_sends(0, i)
        wait_sends(1, i)


def combine_kernel(coef_ref, v_ref, w1_ref, w2_ref, out_ref, hess_ref, stage, sem):
    chans, modes_m, modes_k = v_ref.shape
    on_two = jnp.broadcast_to(coef_ref[6:7, 0:1], (OUT_STRIP, modes_k))
    on_one = jnp.broadcast_to(coef_ref[7:8, 0:1], (OUT_STRIP, modes_k))
    on_start = jnp.broadcast_to(coef_ref[8:9, 0:1], (OUT_STRIP, modes_k))
    pieces = [(c, row) for c in range(chans) for row in range(0, modes_m, OUT_ROWS)]

    def copy(i):
        c, row = pieces[i]
        at = (c, pl.ds(row, OUT_ROWS))
        return pltpu.make_async_copy(stage.at[at], out_ref.at[at], sem.at[i])

    for i, (c, row) in enumerate(pieces):

        def strip(j, _, c=c, row=row):
            at = pl.ds(pl.multiple_of(row + j * OUT_STRIP, OUT_STRIP), OUT_STRIP)
            stage[c, at, :] = (
                on_two * w2_ref[c, at, :] + on_one * w1_ref[c, at, :] + on_start * v_ref[c, at, :]
            )
            return 0

        lax.fori_loop(0, OUT_ROWS // OUT_STRIP, strip, 0)
        copy(i).start()
    for i in range(6):
        hess_ref[i] = coef_ref[i, 0]
    for i in range(len(pieces)):
        copy(i).wait()


def on_device(segs, rads, start_vector, coupling, advect):
    shape = start_vector.shape
    chans, modes_m, modes_k = shape[1], shape[3], shape[4]
    vector = start_vector.reshape(chans, modes_m, modes_k)
    couple = coupling.reshape(chans, chans, modes_m, modes_k)
    cells = float(segs * rads * chans * modes_m * modes_k)
    synth_m, anal_m = make_tables(modes_m)
    synth_k, anal_k = make_tables(modes_k)
    group = 16
    two_count = (segs // group) * rads
    field = (chans, modes_m, modes_k)
    count = chans * PARTS
    in_place = lambda value: pltpu.with_memory_space_constraint(value, pltpu.HBM)
    tables = (synth_k, anal_k.T, synth_m.T, anal_m)
    in_hbm = pl.BlockSpec(memory_space=pltpu.HBM)
    in_vmem = pl.BlockSpec(memory_space=pltpu.VMEM)
    v, w1, w2, coef = pl.pallas_call(
        functools.partial(steps_kernel, (segs, rads, group), cells),
        out_shape=[jax.ShapeDtypeStruct(field, F32)] * 3 + [jax.ShapeDtypeStruct((16, 128), F32)],
        in_specs=[in_hbm, in_hbm, pl.BlockSpec(memory_space=pltpu.SMEM)] + [in_hbm] * 4,
        out_specs=[in_vmem] * 4,
        scratch_shapes=[
            pltpu.VMEM((chans,) + field, BF16),
            pltpu.VMEM((modes_k, modes_k), BF16),
            pltpu.VMEM((modes_k, modes_k), BF16),
            pltpu.VMEM((modes_m, modes_m), BF16),
            pltpu.VMEM((modes_m, modes_m), BF16),
        ]
        + [pltpu.VMEM(field, BF16)] * 11
        + [
            pltpu.VMEM((modes_m, modes_k), F32),
            pltpu.VMEM((8, 128), F32),
            pltpu.VMEM((group, 8, 128), F32),
            pltpu.VMEM((two_count, 8, 128), F32),
            pltpu.SemaphoreType.DMA((5,)),
            pltpu.SemaphoreType.DMA((count,)),
            pltpu.SemaphoreType.DMA((2, 3, count)),
            pltpu.SemaphoreType.DMA((2, 3, count)),
            pltpu.SemaphoreType.DMA((2, 2, count)),
            pltpu.SemaphoreType.DMA((2, count)),
            pltpu.SemaphoreType.DMA((2, 16)),
            pltpu.SemaphoreType.DMA((2, 16)),
        ],
        compiler_params=pltpu.CompilerParams(
            collective_id=0, has_side_effects=True, vmem_limit_bytes=VMEM_LIMIT
        ),
    )(in_place(vector), in_place(couple), advect, *map(in_place, tables))
    out, hess = pl.pallas_call(
        combine_kernel,
        out_shape=(jax.ShapeDtypeStruct(field, F32), jax.ShapeDtypeStruct((6,), F32)),
        in_specs=[in_vmem] * 4,
        out_specs=(in_hbm, pl.BlockSpec(memory_space=pltpu.SMEM)),
        scratch_shapes=[
            pltpu.VMEM(field, F32),
            pltpu.SemaphoreType.DMA((chans * modes_m // OUT_ROWS,)),
        ],
        compiler_params=pltpu.CompilerParams(vmem_limit_bytes=VMEM_LIMIT),
    )(coef, v, w1, w2)
    return out.reshape(shape), hess


def solution(mesh):
    return jax.shard_map(
        functools.partial(on_device, mesh.shape["seg"], mesh.shape["rad"]),
        mesh=mesh,
        in_specs=(
            P("seg", None, "rad", None, None),
            P("seg", None, None, "rad", None, None),
            P("rad"),
        ),
        out_specs=(P("seg", None, "rad", None, None), P()),
        check_vma=False,
    )
```

```python
import functools
import math

import jax
import jax.numpy as jnp
import numpy as np
from jax import lax
from jax.experimental import pallas as pl
from jax.experimental.pallas import tpu as pltpu
from jax.sharding import PartitionSpec as P

RADIAL_ALL = 256
WINDOW_START = 124
RADIAL_GAIN = 0.25
VISC_AXIAL = 4.0
VISC_TURN = 0.05

MESH = pl.DeviceIdType.MESH
F32 = jnp.float32
BF16 = jnp.bfloat16
PARTS = 2
STRIP = 16
TILE = 256
LINE = 4
REACH = (1, 2, 4)
FAR_FIRST = (
    (8, 7, 9, 6, 10, 5, 11, 4, 12, 3, 13, 2, 14, 1, 15),
    (10, 6, 9, 7, 8, 11, 5, 2, 14, 3, 13, 12, 4, 1, 15),
)
OUT_ROWS = 96
OUT_STRIP = 32
VMEM_LIMIT = 34 * 1024 * 1024


def make_tables(count):
    index = np.arange(count)
    half = count // 2
    freq = np.where(index <= half, index, index - half)
    angle = 2.0 * np.pi / count * (freq[:, None] * index[None, :] % count)
    synth = np.where((index <= half)[:, None], np.cos(angle), np.sin(angle))
    weight = np.where((index == 0) | (index == half), 1.0 / count, 2.0 / count)
    analysis = weight[:, None] * synth
    as_bf16 = lambda table: jnp.asarray(table.astype(np.float32).astype(jnp.bfloat16))
    return as_bf16(synth), as_bf16(analysis)


def fold(value):
    total = None
    for row in range(0, value.shape[0], 8):
        for lane in range(0, value.shape[1], 128):
            piece = value[row : row + 8, lane : lane + 128]
            total = piece if total is None else total + piece
    return total


def dot(left, right):
    return jnp.dot(left, right, preferred_element_type=F32)


def steps_kernel(
    sizes, cells,
    v_hbm, couple_hbm, advect_ref, synth_k_hbm, anal_k_hbm, synth_m_hbm, anal_m_hbm,
    v_buf, w1_buf, spec, coef_ref,
    couple, synth_k, anal_k, synth_m, anal_m,
    sent_a, sent_b, low_a, high_a, next_a, low_b, high_b, next_b,
    relay_a, relay_b, mixed, inv_div, slots_one, slots_two,
    load_sem, v_sem,
    send_sem, recv_sem, hop_send, hop_recv, sum_send, sum_recv, met_sem,
):
    segs, rads, group = sizes
    chans, modes_m, modes_k = v_buf.shape
    rows = modes_m // PARTS
    pieces = [(c, q) for c in range(chans) for q in range(PARTS)]
    seg = lax.axis_index("seg")
    rad = lax.axis_index("rad")
    seg_prev = lax.rem(seg + segs - 1, segs)
    seg_next = lax.rem(seg + 1, segs)
    base = (seg // group) * group
    one_me = seg - base
    spread = segs // group
    two_count = spread * rads
    two_me = (seg // group) * rads + rad

    def one_peer(d):
        return lax.rem(one_me + d, group)

    def two_peer(d):
        other = lax.rem(two_me + d, two_count)
        return other, ((other // rads) * group + one_me, lax.rem(other, rads))

    upper_half = seg // group
    column, line = rad // LINE, lax.rem(rad, LINE)
    far_rad = (1 - column) * LINE + line
    detoured = ((line == LINE - 1) & (column == 0)) | ((line == 0) & (column == 1))
    is_source = (one_me == 0) & detoured
    is_sink = (one_me == group - 1) & detoured
    is_relay = (one_me == 1) & (((line == LINE - 1) & (column == 1)) | ((line == 0) & (column == 0)))
    relay = ((1 - upper_half) * group + 1, far_rad)
    relayed_source = ((1 - upper_half) * group, far_rad)
    relayed_sink = (base + group - 1, far_rad)

    loads = [
        pltpu.make_async_copy(source, target, load_sem.at[i])
        for i, (source, target) in enumerate(
            [
                (synth_k_hbm, synth_k),
                (synth_m_hbm, synth_m),
                (couple_hbm, couple),
                (anal_k_hbm, anal_k),
                (anal_m_hbm, anal_m),
            ]
        )
    ]
    v_loads = []
    for i, (c, q) in enumerate(pieces):
        at = (c, pl.ds(q * rows, rows))
        v_loads.append(pltpu.make_async_copy(v_hbm.at[at], v_buf.at[at], v_sem.at[i]))
        v_loads[-1].start()

    barrier = pltpu.get_barrier_semaphore()

    def ring(which, offset):
        if which == 0:
            return base + lax.rem(one_me + group + offset, group), rad
        return two_peer(two_count + offset)[1]

    def signal(device):
        pl.semaphore_signal(barrier, inc=1, device_id=device, device_id_type=MESH)

    for other in (seg_prev, seg_next):
        signal((other, rad))
    for which in range(2):
        signal(ring(which, 1))
        signal(ring(which, -1))

    @pl.when(is_source)
    def _():
        signal(relay)

    @pl.when(is_sink)
    def _():
        signal((base + 1, far_rad))

    @pl.when(is_relay)
    def _():
        signal(relayed_source)
        signal(relayed_sink)

    for load in loads:
        load.start()

    def say_met(step):
        for which in range(2):
            for offset in (REACH[step], -REACH[step]):
                pl.semaphore_signal(met_sem.at[which, step], inc=1, device_id=ring(which, offset), device_id_type=MESH)

    def wait_met(step):
        for which in range(2):
            pl.semaphore_wait(met_sem.at[which, step], 2)

    def sends(phase, i):
        c, q = pieces[i]
        at = (c, pl.ds(q * rows, rows))
        source = (sent_a, sent_b)[phase]
        low, high, nxt = ((low_a, high_a, next_a), (low_b, high_b, next_b))[phase]

        def copy(way, target, device):
            return pltpu.make_async_remote_copy(
                src_ref=source.at[at], dst_ref=target.at[at],
                send_sem=send_sem.at[phase, way, i], recv_sem=recv_sem.at[phase, way, i],
                device_id=device, device_id_type=MESH,
            )

        return (
            copy(0, low, (seg, lax.rem(rad + 1, rads))),
            copy(1, high, (seg, lax.rem(rad + rads - 1, rads))),
            copy(2, nxt, (seg_prev, rad)),
        )

    def hop(phase, i):
        c, q = pieces[i]
        at = (c, pl.ds(q * rows, rows))
        return pltpu.make_async_remote_copy(
            src_ref=(sent_a, sent_b)[phase].at[at], dst_ref=(relay_a, relay_b)[phase].at[at],
            send_sem=hop_send.at[phase, 0, i], recv_sem=hop_recv.at[phase, i],
            device_id=relay, device_id_type=MESH,
        )

    def onward(phase, i):
        c, q = pieces[i]
        at = (c, pl.ds(q * rows, rows))
        return pltpu.make_async_remote_copy(
            src_ref=(relay_a, relay_b)[phase].at[at], dst_ref=(next_a, next_b)[phase].at[at],
            send_sem=hop_send.at[phase, 1, i], recv_sem=recv_sem.at[phase, 2, i],
            device_id=relayed_sink, device_id_type=MESH,
        )

    def pass_on(phase, i):
        @pl.when(is_relay)
        def _():
            for j in ([0] if i == 0 else []) + ([i + 1] if i + 1 < len(pieces) else []):
                hop(phase, j).wait_recv()
                onward(phase, j).start()

    def start_sends(phase, i):
        up, down, back = sends(phase, i)

        @pl.when(rad < rads - 1)
        def _():
            up.start()

        @pl.when(rad > 0)
        def _():
            down.start()

        @pl.when(is_source)
        def _():
            hop(phase, i).start()

        @pl.when(jnp.logical_not(is_source))
        def _():
            back.start()

    def wait_recvs(phase, i):
        up, down, back = sends(phase, i)

        @pl.when(rad > 0)
        def _():
            up.wait_recv()

        @pl.when(rad < rads - 1)
        def _():
            down.wait_recv()

        back.wait_recv()

    def wait_sends(phase, i):
        up, down, back = sends(phase, i)

        @pl.when(rad < rads - 1)
        def _():
            up.wait_send()

        @pl.when(rad > 0)
        def _():
            down.wait_send()

        @pl.when(is_source)
        def _():
            hop(phase, i).wait_send()

        @pl.when(jnp.logical_not(is_source))
        def _():
            back.wait_send()

        @pl.when(is_relay)
        def _():
            onward(phase, i).wait_send()

    def strips(c, q, body, carry):
        def step(j, carry):
            row = pl.multiple_of(q * rows + j * STRIP, STRIP)
            return body(row, pl.ds(row, STRIP), carry)

        return lax.fori_loop(0, rows // STRIP, step, carry)

    zero = jnp.zeros((8, 128), F32)
    gram = [zero] * 6
    for i, (c, q) in enumerate(pieces):
        v_loads[i].wait()

        def rounding(row, at, total, c=c):
            value = v_buf[c, at, :]
            sent_a[c, at, :] = value.astype(BF16)
            return total + fold(value * value)

        gram[0] = strips(c, q, rounding, gram[0])
        if i == 0:
            extra = jnp.where(is_relay, 2, jnp.where(is_source | is_sink, 1, 0))
            pl.semaphore_wait(barrier, 6 + extra)
        start_sends(0, i)

    @pl.when(rad == 0)
    def _():
        low_a[...] = jnp.zeros_like(low_a)
        low_b[...] = jnp.zeros_like(low_b)

    @pl.when(rad == rads - 1)
    def _():
        high_a[...] = jnp.zeros_like(high_a)
        high_b[...] = jnp.zeros_like(high_b)

    say_met(0)

    def freq(index, count):
        return jnp.where(index <= count // 2, index, index - count // 2).astype(F32)

    freq_k = freq(lax.broadcasted_iota(jnp.int32, (1, modes_k), 1), modes_k)
    axial = VISC_AXIAL * (freq_k / (modes_k // 2)) ** 2
    mode = lax.broadcasted_iota(jnp.int32, (1, modes_k), 1)
    half = modes_k // 2
    wavenum = jnp.where(mode < half, mode, half - mode).astype(F32) * advect_ref[0]
    radius = (jnp.full((1, modes_k), rad + WINDOW_START, jnp.int32).astype(F32) + 0.5) / RADIAL_ALL

    def divide(j, _):
        row = pl.multiple_of(j * STRIP, STRIP)
        freq_m = freq(row + lax.broadcasted_iota(jnp.int32, (STRIP, modes_k), 0), modes_m)
        turning = (freq_m / (modes_m // 2)) ** 2
        inv_div[pl.ds(row, STRIP), :] = 1.0 / (1.0 + axial + VISC_TURN * turning / (radius * radius))
        return 0

    lax.fori_loop(0, modes_m // STRIP, divide, 0)

    def spectral(source):
        def synthesis(j, _):
            at = pl.ds(pl.multiple_of(j * TILE, TILE), TILE)
            physical = [
                dot(synth_m[...], dot(source[c], synth_k[:, at]).astype(BF16)) for c in range(chans)
            ]
            for c in range(chans):
                total = couple[c, 0, :, at].astype(F32) * physical[0]
                for k in range(1, chans):
                    total += couple[c, k, :, at].astype(F32) * physical[k]
                mixed[c, :, at] = total.astype(BF16)
            return 0

        lax.fori_loop(0, modes_k // TILE, synthesis, 0)

        def analysis(step, _):
            c = step // (modes_k // TILE)
            j = lax.rem(step, modes_k // TILE)
            at = pl.ds(pl.multiple_of(j * TILE, TILE), TILE)
            section = dot(mixed[c], anal_k[:, at]).astype(BF16)
            spec[c, :, at] = dot(anal_m[...], section)
            return 0

        lax.fori_loop(0, chans * (modes_k // TILE), analysis, 0)

    def image(field, bufs, c, at):
        sent, low, high, nxt = bufs
        swapped = jnp.concatenate([field[:, half:], field[:, :half]], axis=1)
        outer = low[c, at, :].astype(F32) + high[c, at, :].astype(F32)
        radial = RADIAL_GAIN * (outer - 2.0 * sent[c, at, :].astype(F32))
        total = field + spec[c, at, :] - wavenum * swapped + radial
        return total * inv_div[at, :] - nxt[c, at, :].astype(F32)

    for load in loads:
        load.wait()
    spectral(sent_a)
    wait_met(0)
    say_met(1)

    for i, (c, q) in enumerate(pieces):
        pass_on(0, i)
        wait_recvs(0, i)

        def first(row, at, totals, c=c):
            field = v_buf[c, at, :]
            value = image(field, (sent_a, low_a, high_a, next_a), c, at)
            w1_buf[c, at, :] = value
            sent_b[c, at, :] = value.astype(BF16)
            return totals[0] + fold(value * field), totals[1] + fold(value * value)

        gram[1], gram[2] = strips(c, q, first, (gram[1], gram[2]))
        start_sends(1, i)
        if i == 0:
            wait_met(1)
            say_met(2)
    wait_met(2)

    spectral(sent_b)

    for i, (c, q) in enumerate(pieces):
        pass_on(1, i)
        wait_sends(0, i)
        wait_recvs(1, i)

        def second(row, at, totals, c=c):
            field = w1_buf[c, at, :]
            value = image(field, (sent_b, low_b, high_b, next_b), c, at)
            spec[c, at, :] = value
            return (
                totals[0] + fold(value * v_buf[c, at, :]),
                totals[1] + fold(value * field),
                totals[2] + fold(value * value),
            )

        gram[3], gram[4], gram[5] = strips(c, q, second, (gram[3], gram[4], gram[5]))

    here = lax.broadcasted_iota(jnp.int32, (8, 128), 0) == lax.broadcasted_iota(jnp.int32, (8, 128), 1)
    rows_of = jnp.concatenate([jnp.sum(value, axis=0, keepdims=True) for value in gram] + [zero[:2]], axis=0)
    mine = jnp.sum(jnp.where(here, jnp.sum(rows_of, axis=1, keepdims=True), 0.0), axis=0, keepdims=True)
    stages = (
        (slots_one, one_me, group, lambda d: (base + one_peer(d), rad)),
        (slots_two, two_me, two_count, lambda d: two_peer(d)[1]),
    )

    def message(stage, d, slot):
        slots, _, _, peer = stages[stage]
        return pltpu.make_async_remote_copy(
            src_ref=slots.at[slot], dst_ref=slots.at[slot],
            send_sem=sum_send.at[stage, d], recv_sem=sum_recv.at[stage, d],
            device_id=peer(d), device_id_type=MESH,
        )

    def send_sums(stage, value):
        slots, me, _, _ = stages[stage]
        slots[me] = value
        for d in FAR_FIRST[stage]:
            message(stage, d, me).start()

    def total_of(stage):
        slots, me, count, _ = stages[stage]
        for d in FAR_FIRST[stage][::-1]:
            message(stage, d, lax.rem(me + count - d, count)).wait_recv()
        total = slots[0]
        for slot in range(1, count):
            total = total + slots[slot]
        return total

    def sums_sent(stage):
        for d in FAR_FIRST[stage]:
            message(stage, d, stages[stage][1]).wait_send()

    send_sums(0, mine)
    for i in range(len(pieces)):
        wait_sends(1, i)
    partial = total_of(0)
    send_sums(1, partial)
    sums_sent(0)
    sums = jnp.broadcast_to(total_of(1), (8, 128))
    sums = jnp.sum(jnp.where(here, sums, 0.0), axis=1, keepdims=True) * (1.0 / cells)
    sums = jnp.broadcast_to(sums, (8, 128))
    g00, g01, g11, g02, g12, g22 = (sums[i : i + 1] for i in range(6))
    start_norm = jnp.sqrt(g00)
    upper_one = g01 / g00
    lower_one = jnp.sqrt(g11 / g00 - upper_one * upper_one)
    scale = start_norm * lower_one
    upper_two = (g02 - upper_one * g01) / (g00 * lower_one)
    middle_two = (g12 - upper_one * (g02 + g11) + upper_one * upper_one * g01) / (scale * scale)
    length = (g22 - 2.0 * upper_one * g12 + upper_one * upper_one * g11) / (scale * scale)
    lower_two = jnp.sqrt(length - upper_two * upper_two - middle_two * middle_two)
    on_two = 1.0 / (scale * lower_two)
    on_one = -(upper_one + middle_two) * on_two
    on_start = (middle_two * upper_one / scale - upper_two / start_norm) / lower_two
    coef_ref[0:8, :] = jnp.concatenate(
        [start_norm, upper_one, lower_one, upper_two, middle_two, lower_two, on_two, on_one], axis=0
    )
    coef_ref[8:16, :] = jnp.broadcast_to(on_start, (8, 128))

    sums_sent(1)


def combine_kernel(coef_ref, v_ref, w1_ref, w2_ref, out_ref, hess_ref, stage, sem):
    chans, modes_m, modes_k = v_ref.shape
    on_two = jnp.broadcast_to(coef_ref[6:7, 0:1], (OUT_STRIP, modes_k))
    on_one = jnp.broadcast_to(coef_ref[7:8, 0:1], (OUT_STRIP, modes_k))
    on_start = jnp.broadcast_to(coef_ref[8:9, 0:1], (OUT_STRIP, modes_k))
    pieces = [(c, row) for c in range(chans) for row in range(0, modes_m, OUT_ROWS)]

    def copy(i):
        c, row = pieces[i]
        at = (c, pl.ds(row, OUT_ROWS))
        return pltpu.make_async_copy(stage.at[at], out_ref.at[at], sem.at[i])

    for i, (c, row) in enumerate(pieces):

        def strip(j, _, c=c, row=row):
            at = pl.ds(pl.multiple_of(row + j * OUT_STRIP, OUT_STRIP), OUT_STRIP)
            stage[c, at, :] = (
                on_two * w2_ref[c, at, :] + on_one * w1_ref[c, at, :] + on_start * v_ref[c, at, :]
            )
            return 0

        lax.fori_loop(0, OUT_ROWS // OUT_STRIP, strip, 0)
        copy(i).start()
    for i in range(6):
        hess_ref[i] = coef_ref[i, 0]
    for i in range(len(pieces)):
        copy(i).wait()


def on_device(segs, rads, start_vector, coupling, advect):
    shape = start_vector.shape
    chans, modes_m, modes_k = shape[1], shape[3], shape[4]
    vector = start_vector.reshape(chans, modes_m, modes_k)
    couple = coupling.reshape(chans, chans, modes_m, modes_k)
    cells = float(segs * rads * chans * modes_m * modes_k)
    synth_m, anal_m = make_tables(modes_m)
    synth_k, anal_k = make_tables(modes_k)
    group = 16
    two_count = (segs // group) * rads
    field = (chans, modes_m, modes_k)
    count = chans * PARTS
    in_place = lambda value: pltpu.with_memory_space_constraint(value, pltpu.HBM)
    tables = (synth_k, anal_k.T, synth_m.T, anal_m)
    in_hbm = pl.BlockSpec(memory_space=pltpu.HBM)
    in_vmem = pl.BlockSpec(memory_space=pltpu.VMEM)
    v, w1, w2, coef = pl.pallas_call(
        functools.partial(steps_kernel, (segs, rads, group), cells),
        out_shape=[jax.ShapeDtypeStruct(field, F32)] * 3 + [jax.ShapeDtypeStruct((16, 128), F32)],
        in_specs=[in_hbm, in_hbm, pl.BlockSpec(memory_space=pltpu.SMEM)] + [in_hbm] * 4,
        out_specs=[in_vmem] * 4,
        scratch_shapes=[
            pltpu.VMEM((chans,) + field, BF16),
            pltpu.VMEM((modes_k, modes_k), BF16),
            pltpu.VMEM((modes_k, modes_k), BF16),
            pltpu.VMEM((modes_m, modes_m), BF16),
            pltpu.VMEM((modes_m, modes_m), BF16),
        ]
        + [pltpu.VMEM(field, BF16)] * 11
        + [
            pltpu.VMEM((modes_m, modes_k), F32),
            pltpu.VMEM((group, 1, 128), F32),
            pltpu.VMEM((two_count, 1, 128), F32),
            pltpu.SemaphoreType.DMA((5,)),
            pltpu.SemaphoreType.DMA((count,)),
            pltpu.SemaphoreType.DMA((2, 3, count)),
            pltpu.SemaphoreType.DMA((2, 3, count)),
            pltpu.SemaphoreType.DMA((2, 2, count)),
            pltpu.SemaphoreType.DMA((2, count)),
            pltpu.SemaphoreType.DMA((2, 16)),
            pltpu.SemaphoreType.DMA((2, 16)),
            pltpu.SemaphoreType.REGULAR((2, len(REACH))),
        ],
        compiler_params=pltpu.CompilerParams(
            collective_id=0, has_side_effects=True, vmem_limit_bytes=VMEM_LIMIT
        ),
    )(in_place(vector), in_place(couple), advect, *map(in_place, tables))
    out, hess = pl.pallas_call(
        combine_kernel,
        out_shape=(jax.ShapeDtypeStruct(field, F32), jax.ShapeDtypeStruct((6,), F32)),
        in_specs=[in_vmem] * 4,
        out_specs=(in_hbm, pl.BlockSpec(memory_space=pltpu.SMEM)),
        scratch_shapes=[
            pltpu.VMEM(field, F32),
            pltpu.SemaphoreType.DMA((chans * modes_m // OUT_ROWS,)),
        ],
        compiler_params=pltpu.CompilerParams(vmem_limit_bytes=VMEM_LIMIT),
    )(coef, v, w1, w2)
    return out.reshape(shape), hess


def solution(mesh):
    return jax.shard_map(
        functools.partial(on_device, mesh.shape["seg"], mesh.shape["rad"]),
        mesh=mesh,
        in_specs=(
            P("seg", None, "rad", None, None),
            P("seg", None, None, "rad", None, None),
            P("rad"),
        ),
        out_specs=(P("seg", None, "rad", None, None), P()),
        check_vma=False,
    )
```

```python
import functools
import math

import jax
import jax.numpy as jnp
import numpy as np
from jax import lax
from jax.experimental import pallas as pl
from jax.experimental.pallas import tpu as pltpu
from jax.sharding import PartitionSpec as P

RADIAL_ALL = 256
WINDOW_START = 124
RADIAL_GAIN = 0.25
VISC_AXIAL = 4.0
VISC_TURN = 0.05

MESH = pl.DeviceIdType.MESH
F32 = jnp.float32
BF16 = jnp.bfloat16
PARTS = 2
STRIP = 16
TILE = 256
LINE = 4
REACH = (1, 2, 4)
FAR_FIRST = (
    (8, 7, 9, 6, 10, 5, 11, 4, 12, 3, 13, 2, 14, 1, 15),
    (10, 6, 9, 7, 8, 11, 5, 2, 14, 3, 13, 12, 4, 1, 15),
)
OUT_ROWS = 96
OUT_STRIP = 32
VMEM_LIMIT = 34 * 1024 * 1024


def make_tables(count):
    index = np.arange(count)
    half = count // 2
    freq = np.where(index <= half, index, index - half)
    angle = 2.0 * np.pi / count * (freq[:, None] * index[None, :] % count)
    synth = np.where((index <= half)[:, None], np.cos(angle), np.sin(angle))
    weight = np.where((index == 0) | (index == half), 1.0 / count, 2.0 / count)
    analysis = weight[:, None] * synth
    as_bf16 = lambda table: jnp.asarray(table.astype(np.float32).astype(jnp.bfloat16))
    return as_bf16(synth), as_bf16(analysis)


def fold(value):
    total = None
    for row in range(0, value.shape[0], 8):
        for lane in range(0, value.shape[1], 128):
            piece = value[row : row + 8, lane : lane + 128]
            total = piece if total is None else total + piece
    return total


def dot(left, right):
    return jnp.dot(left, right, preferred_element_type=F32)


def steps_kernel(
    sizes, cells,
    v_hbm, couple_hbm, advect_ref, synth_k_hbm, anal_k_hbm, synth_m_hbm, anal_m_hbm,
    v_buf, w1_buf, spec, coef_ref,
    couple, synth_k, anal_k, synth_m, anal_m,
    sent_a, sent_b, low_a, high_a, next_a, low_b, high_b, next_b,
    relay_a, relay_b, mixed, inv_div, slots_one, slots_two,
    load_sem, v_sem,
    send_sem, recv_sem, hop_send, hop_recv, sum_send, sum_recv, met_sem,
):
    segs, rads, group = sizes
    chans, modes_m, modes_k = v_buf.shape
    rows = modes_m // PARTS
    pieces = [(c, q) for c in range(chans) for q in range(PARTS)]
    seg = lax.axis_index("seg")
    rad = lax.axis_index("rad")
    seg_prev = lax.rem(seg + segs - 1, segs)
    seg_next = lax.rem(seg + 1, segs)
    base = (seg // group) * group
    one_me = seg - base
    spread = segs // group
    two_count = spread * rads
    two_me = (seg // group) * rads + rad

    def one_peer(d):
        return lax.rem(one_me + d, group)

    def two_peer(d):
        other = lax.rem(two_me + d, two_count)
        return other, ((other // rads) * group + one_me, lax.rem(other, rads))

    upper_half = seg // group
    column, line = rad // LINE, lax.rem(rad, LINE)
    far_rad = (1 - column) * LINE + line
    detoured = ((line == LINE - 1) & (column == 0)) | ((line == 0) & (column == 1))
    is_source = (one_me == 0) & detoured
    is_sink = (one_me == group - 1) & detoured
    is_relay = (one_me == 1) & (((line == LINE - 1) & (column == 1)) | ((line == 0) & (column == 0)))
    relay = ((1 - upper_half) * group + 1, far_rad)
    relayed_source = ((1 - upper_half) * group, far_rad)
    relayed_sink = (base + group - 1, far_rad)

    loads = [
        pltpu.make_async_copy(source, target, load_sem.at[i])
        for i, (source, target) in enumerate(
            [
                (synth_k_hbm, synth_k),
                (synth_m_hbm, synth_m),
                (couple_hbm, couple),
                (anal_k_hbm, anal_k),
                (anal_m_hbm, anal_m),
            ]
        )
    ]
    v_loads = []
    for i, (c, q) in enumerate(pieces):
        at = (c, pl.ds(q * rows, rows))
        v_loads.append(pltpu.make_async_copy(v_hbm.at[at], v_buf.at[at], v_sem.at[i]))
        v_loads[-1].start()

    barrier = pltpu.get_barrier_semaphore()

    def ring(which, offset):
        if which == 0:
            return base + lax.rem(one_me + group + offset, group), rad
        return two_peer(two_count + offset)[1]

    def signal(device):
        pl.semaphore_signal(barrier, inc=1, device_id=device, device_id_type=MESH)

    for other in (seg_prev, seg_next):
        signal((other, rad))
    for which in range(2):
        signal(ring(which, 1))
        signal(ring(which, -1))

    @pl.when(is_source)
    def _():
        signal(relay)

    @pl.when(is_sink)
    def _():
        signal((base + 1, far_rad))

    @pl.when(is_relay)
    def _():
        signal(relayed_source)
        signal(relayed_sink)

    for load in loads:
        load.start()

    def say_met(step):
        for which in range(2):
            for offset in (REACH[step], -REACH[step]):
                pl.semaphore_signal(met_sem.at[which, step], inc=1, device_id=ring(which, offset), device_id_type=MESH)

    def wait_met(step):
        for which in range(2):
            pl.semaphore_wait(met_sem.at[which, step], 2)

    def sends(phase, i):
        c, q = pieces[i]
        at = (c, pl.ds(q * rows, rows))
        source = (sent_a, sent_b)[phase]
        low, high, nxt = ((low_a, high_a, next_a), (low_b, high_b, next_b))[phase]

        def copy(way, target, device):
            return pltpu.make_async_remote_copy(
                src_ref=source.at[at], dst_ref=target.at[at],
                send_sem=send_sem.at[phase, way, i], recv_sem=recv_sem.at[phase, way, i],
                device_id=device, device_id_type=MESH,
            )

        return (
            copy(0, low, (seg, lax.rem(rad + 1, rads))),
            copy(1, high, (seg, lax.rem(rad + rads - 1, rads))),
            copy(2, nxt, (seg_prev, rad)),
        )

    def hop(phase, i):
        c, q = pieces[i]
        at = (c, pl.ds(q * rows, rows))
        return pltpu.make_async_remote_copy(
            src_ref=(sent_a, sent_b)[phase].at[at], dst_ref=(relay_a, relay_b)[phase].at[at],
            send_sem=hop_send.at[phase, 0, i], recv_sem=hop_recv.at[phase, i],
            device_id=relay, device_id_type=MESH,
        )

    def onward(phase, i):
        c, q = pieces[i]
        at = (c, pl.ds(q * rows, rows))
        return pltpu.make_async_remote_copy(
            src_ref=(relay_a, relay_b)[phase].at[at], dst_ref=(next_a, next_b)[phase].at[at],
            send_sem=hop_send.at[phase, 1, i], recv_sem=recv_sem.at[phase, 2, i],
            device_id=relayed_sink, device_id_type=MESH,
        )

    def pass_on(phase, i):
        @pl.when(is_relay)
        def _():
            for j in ([0] if i == 0 else []) + ([i + 1] if i + 1 < len(pieces) else []):
                hop(phase, j).wait_recv()
                onward(phase, j).start()

    def start_sends(phase, i):
        up, down, back = sends(phase, i)

        @pl.when(rad < rads - 1)
        def _():
            up.start()

        @pl.when(rad > 0)
        def _():
            down.start()

        @pl.when(is_source)
        def _():
            hop(phase, i).start()

        @pl.when(jnp.logical_not(is_source))
        def _():
            back.start()

    def wait_recvs(phase, i):
        up, down, back = sends(phase, i)

        @pl.when(rad > 0)
        def _():
            up.wait_recv()

        @pl.when(rad < rads - 1)
        def _():
            down.wait_recv()

        back.wait_recv()

    def wait_sends(phase, i):
        up, down, back = sends(phase, i)

        @pl.when(rad < rads - 1)
        def _():
            up.wait_send()

        @pl.when(rad > 0)
        def _():
            down.wait_send()

        @pl.when(is_source)
        def _():
            hop(phase, i).wait_send()

        @pl.when(jnp.logical_not(is_source))
        def _():
            back.wait_send()

        @pl.when(is_relay)
        def _():
            onward(phase, i).wait_send()

    def strips(c, q, body, carry):
        def step(j, carry):
            row = pl.multiple_of(q * rows + j * STRIP, STRIP)
            return body(row, pl.ds(row, STRIP), carry)

        return lax.fori_loop(0, rows // STRIP, step, carry)

    zero = jnp.zeros((8, 128), F32)
    gram = [zero] * 6
    for i, (c, q) in enumerate(pieces):
        v_loads[i].wait()

        def rounding(row, at, total, c=c):
            value = v_buf[c, at, :]
            sent_a[c, at, :] = value.astype(BF16)
            return total + fold(value * value)

        gram[0] = strips(c, q, rounding, gram[0])
        if i == 0:
            extra = jnp.where(is_relay, 2, jnp.where(is_source | is_sink, 1, 0))
            pl.semaphore_wait(barrier, 6 + extra)
        start_sends(0, i)

    @pl.when(rad == 0)
    def _():
        low_a[...] = jnp.zeros_like(low_a)
        low_b[...] = jnp.zeros_like(low_b)

    @pl.when(rad == rads - 1)
    def _():
        high_a[...] = jnp.zeros_like(high_a)
        high_b[...] = jnp.zeros_like(high_b)

    say_met(0)

    def freq(index, count):
        return jnp.where(index <= count // 2, index, index - count // 2).astype(F32)

    freq_k = freq(lax.broadcasted_iota(jnp.int32, (1, modes_k), 1), modes_k)
    axial = VISC_AXIAL * (freq_k / (modes_k // 2)) ** 2
    mode = lax.broadcasted_iota(jnp.int32, (1, modes_k), 1)
    half = modes_k // 2
    wavenum = jnp.where(mode < half, mode, half - mode).astype(F32) * advect_ref[0]
    radius = (jnp.full((1, modes_k), rad + WINDOW_START, jnp.int32).astype(F32) + 0.5) / RADIAL_ALL

    def divide(j, _):
        row = pl.multiple_of(j * STRIP, STRIP)
        freq_m = freq(row + lax.broadcasted_iota(jnp.int32, (STRIP, modes_k), 0), modes_m)
        turning = (freq_m / (modes_m // 2)) ** 2
        inv_div[pl.ds(row, STRIP), :] = 1.0 / (1.0 + axial + VISC_TURN * turning / (radius * radius))
        return 0

    lax.fori_loop(0, modes_m // STRIP, divide, 0)

    def spectral(source):
        def synthesis(j, _):
            at = pl.ds(pl.multiple_of(j * TILE, TILE), TILE)
            physical = [
                dot(synth_m[...], dot(source[c], synth_k[:, at]).astype(BF16)) for c in range(chans)
            ]
            for c in range(chans):
                total = couple[c, 0, :, at].astype(F32) * physical[0]
                for k in range(1, chans):
                    total += couple[c, k, :, at].astype(F32) * physical[k]
                mixed[c, :, at] = total.astype(BF16)
            return 0

        lax.fori_loop(0, modes_k // TILE, synthesis, 0)

        def analysis(step, _):
            c = step // (modes_k // TILE)
            j = lax.rem(step, modes_k // TILE)
            at = pl.ds(pl.multiple_of(j * TILE, TILE), TILE)
            section = dot(mixed[c], anal_k[:, at]).astype(BF16)
            spec[c, :, at] = dot(anal_m[...], section)
            return 0

        lax.fori_loop(0, chans * (modes_k // TILE), analysis, 0)

    def image(field, bufs, c, at):
        sent, low, high, nxt = bufs
        swapped = jnp.concatenate([field[:, half:], field[:, :half]], axis=1)
        outer = low[c, at, :].astype(F32) + high[c, at, :].astype(F32)
        radial = RADIAL_GAIN * (outer - 2.0 * sent[c, at, :].astype(F32))
        total = field + spec[c, at, :] - wavenum * swapped + radial
        return total * inv_div[at, :] - nxt[c, at, :].astype(F32)

    for load in loads:
        load.wait()
    spectral(sent_a)
    wait_met(0)
    say_met(1)

    for i, (c, q) in enumerate(pieces):
        pass_on(0, i)
        wait_recvs(0, i)

        def first(row, at, totals, c=c):
            field = v_buf[c, at, :]
            value = image(field, (sent_a, low_a, high_a, next_a), c, at)
            w1_buf[c, at, :] = value
            sent_b[c, at, :] = value.astype(BF16)
            return totals[0] + fold(value * field), totals[1] + fold(value * value)

        gram[1], gram[2] = strips(c, q, first, (gram[1], gram[2]))
        start_sends(1, i)
        if i == 0:
            wait_met(1)
            say_met(2)
    wait_met(2)

    spectral(sent_b)

    for i, (c, q) in enumerate(pieces):
        pass_on(1, i)
        wait_sends(0, i)
        wait_recvs(1, i)

        def second(row, at, totals, c=c):
            field = w1_buf[c, at, :]
            value = image(field, (sent_b, low_b, high_b, next_b), c, at)
            spec[c, at, :] = value
            return (
                totals[0] + fold(value * v_buf[c, at, :]),
                totals[1] + fold(value * field),
                totals[2] + fold(value * value),
            )

        gram[3], gram[4], gram[5] = strips(c, q, second, (gram[3], gram[4], gram[5]))

    here = lax.broadcasted_iota(jnp.int32, (8, 128), 0) == lax.broadcasted_iota(jnp.int32, (8, 128), 1)
    rows_of = jnp.concatenate([jnp.sum(value, axis=0, keepdims=True) for value in gram] + [zero[:2]], axis=0)
    mine = jnp.sum(jnp.where(here, jnp.sum(rows_of, axis=1, keepdims=True), 0.0), axis=0, keepdims=True)
    stages = (
        (slots_one, one_me, group, lambda d: (base + one_peer(d), rad)),
        (slots_two, two_me, two_count, lambda d: two_peer(d)[1]),
    )

    def message(stage, d, slot):
        slots, _, _, peer = stages[stage]
        return pltpu.make_async_remote_copy(
            src_ref=slots.at[slot], dst_ref=slots.at[slot],
            send_sem=sum_send.at[stage, d], recv_sem=sum_recv.at[stage, d],
            device_id=peer(d), device_id_type=MESH,
        )

    def send_sums(stage, value):
        slots, me, _, _ = stages[stage]
        slots[me] = value
        for d in FAR_FIRST[stage]:
            message(stage, d, me).start()

    def total_of(stage):
        slots, me, count, _ = stages[stage]
        for d in FAR_FIRST[stage][::-1]:
            message(stage, d, lax.rem(me + count - d, count)).wait_recv()
        total = slots[0]
        for slot in range(1, count):
            total = total + slots[slot]
        return total

    def sums_sent(stage):
        for d in FAR_FIRST[stage]:
            message(stage, d, stages[stage][1]).wait_send()

    send_sums(0, mine)
    for i in range(len(pieces)):
        wait_sends(1, i)
    partial = total_of(0)
    send_sums(1, partial)
    sums_sent(0)
    sums = jnp.broadcast_to(total_of(1), (8, 128))
    sums = jnp.sum(jnp.where(here, sums, 0.0), axis=1, keepdims=True) * (1.0 / cells)
    sums = jnp.broadcast_to(sums, (8, 128))
    g00, g01, g11, g02, g12, g22 = (sums[i : i + 1] for i in range(6))
    by_start = 1.0 / g00
    upper_one = g01 * by_start
    rest_one = g11 - upper_one * g01
    by_rest = 1.0 / rest_one
    along_start = g02 - upper_one * g01
    along_rest = g12 - upper_one * (g02 + g11) + upper_one * upper_one * g01
    length = g22 - 2.0 * upper_one * g12 + upper_one * upper_one * g11
    middle_two = along_rest * by_rest
    start_part = along_start * by_start
    rest_two = length - along_start * start_part - along_rest * middle_two
    on_two = 1.0 / jnp.sqrt(rest_two)
    on_one = -(upper_one + middle_two) * on_two
    on_start = (upper_one * middle_two - start_part) * on_two
    start_norm = jnp.sqrt(g00)
    lower_one = jnp.sqrt(rest_one * by_start)
    upper_two = start_part / lower_one
    lower_two = jnp.sqrt(rest_two * by_rest)
    coef_ref[0:8, :] = jnp.concatenate(
        [start_norm, upper_one, lower_one, upper_two, middle_two, lower_two, on_two, on_one], axis=0
    )
    coef_ref[8:16, :] = jnp.broadcast_to(on_start, (8, 128))

    sums_sent(1)


def combine_kernel(coef_ref, v_ref, w1_ref, w2_ref, out_ref, hess_ref, stage, sem):
    chans, modes_m, modes_k = v_ref.shape
    on_two = jnp.broadcast_to(coef_ref[6:7, 0:1], (OUT_STRIP, modes_k))
    on_one = jnp.broadcast_to(coef_ref[7:8, 0:1], (OUT_STRIP, modes_k))
    on_start = jnp.broadcast_to(coef_ref[8:9, 0:1], (OUT_STRIP, modes_k))
    pieces = [(c, row) for c in range(chans) for row in range(0, modes_m, OUT_ROWS)]

    def copy(i):
        c, row = pieces[i]
        at = (c, pl.ds(row, OUT_ROWS))
        return pltpu.make_async_copy(stage.at[at], out_ref.at[at], sem.at[i])

    for i, (c, row) in enumerate(pieces):

        def strip(j, _, c=c, row=row):
            at = pl.ds(pl.multiple_of(row + j * OUT_STRIP, OUT_STRIP), OUT_STRIP)
            stage[c, at, :] = (
                on_two * w2_ref[c, at, :] + on_one * w1_ref[c, at, :] + on_start * v_ref[c, at, :]
            )
            return 0

        lax.fori_loop(0, OUT_ROWS // OUT_STRIP, strip, 0)
        copy(i).start()
    for i in range(6):
        hess_ref[i] = coef_ref[i, 0]
    for i in range(len(pieces)):
        copy(i).wait()


def on_device(segs, rads, start_vector, coupling, advect):
    shape = start_vector.shape
    chans, modes_m, modes_k = shape[1], shape[3], shape[4]
    vector = start_vector.reshape(chans, modes_m, modes_k)
    couple = coupling.reshape(chans, chans, modes_m, modes_k)
    cells = float(segs * rads * chans * modes_m * modes_k)
    synth_m, anal_m = make_tables(modes_m)
    synth_k, anal_k = make_tables(modes_k)
    group = 16
    two_count = (segs // group) * rads
    field = (chans, modes_m, modes_k)
    count = chans * PARTS
    in_place = lambda value: pltpu.with_memory_space_constraint(value, pltpu.HBM)
    tables = (synth_k, anal_k.T, synth_m.T, anal_m)
    in_hbm = pl.BlockSpec(memory_space=pltpu.HBM)
    in_vmem = pl.BlockSpec(memory_space=pltpu.VMEM)
    v, w1, w2, coef = pl.pallas_call(
        functools.partial(steps_kernel, (segs, rads, group), cells),
        out_shape=[jax.ShapeDtypeStruct(field, F32)] * 3 + [jax.ShapeDtypeStruct((16, 128), F32)],
        in_specs=[in_hbm, in_hbm, pl.BlockSpec(memory_space=pltpu.SMEM)] + [in_hbm] * 4,
        out_specs=[in_vmem] * 4,
        scratch_shapes=[
            pltpu.VMEM((chans,) + field, BF16),
            pltpu.VMEM((modes_k, modes_k), BF16),
            pltpu.VMEM((modes_k, modes_k), BF16),
            pltpu.VMEM((modes_m, modes_m), BF16),
            pltpu.VMEM((modes_m, modes_m), BF16),
        ]
        + [pltpu.VMEM(field, BF16)] * 11
        + [
            pltpu.VMEM((modes_m, modes_k), F32),
            pltpu.VMEM((group, 1, 128), F32),
            pltpu.VMEM((two_count, 1, 128), F32),
            pltpu.SemaphoreType.DMA((5,)),
            pltpu.SemaphoreType.DMA((count,)),
            pltpu.SemaphoreType.DMA((2, 3, count)),
            pltpu.SemaphoreType.DMA((2, 3, count)),
            pltpu.SemaphoreType.DMA((2, 2, count)),
            pltpu.SemaphoreType.DMA((2, count)),
            pltpu.SemaphoreType.DMA((2, 16)),
            pltpu.SemaphoreType.DMA((2, 16)),
            pltpu.SemaphoreType.REGULAR((2, len(REACH))),
        ],
        compiler_params=pltpu.CompilerParams(
            collective_id=0, has_side_effects=True, vmem_limit_bytes=VMEM_LIMIT
        ),
    )(in_place(vector), in_place(couple), advect, *map(in_place, tables))
    out, hess = pl.pallas_call(
        combine_kernel,
        out_shape=(jax.ShapeDtypeStruct(field, F32), jax.ShapeDtypeStruct((6,), F32)),
        in_specs=[in_vmem] * 4,
        out_specs=(in_hbm, pl.BlockSpec(memory_space=pltpu.SMEM)),
        scratch_shapes=[
            pltpu.VMEM(field, F32),
            pltpu.SemaphoreType.DMA((chans * modes_m // OUT_ROWS,)),
        ],
        compiler_params=pltpu.CompilerParams(vmem_limit_bytes=VMEM_LIMIT),
    )(coef, v, w1, w2)
    return out.reshape(shape), hess


def solution(mesh):
    return jax.shard_map(
        functools.partial(on_device, mesh.shape["seg"], mesh.shape["rad"]),
        mesh=mesh,
        in_specs=(
            P("seg", None, "rad", None, None),
            P("seg", None, None, "rad", None, None),
            P("rad"),
        ),
        out_specs=(P("seg", None, "rad", None, None), P()),
        check_vma=False,
    )
```

```python
import functools
import math

import jax
import jax.numpy as jnp
import numpy as np
from jax import lax
from jax.experimental import pallas as pl
from jax.experimental.pallas import tpu as pltpu
from jax.sharding import PartitionSpec as P

RADIAL_ALL = 256
WINDOW_START = 124
RADIAL_GAIN = 0.25
VISC_AXIAL = 4.0
VISC_TURN = 0.05

MESH = pl.DeviceIdType.MESH
F32 = jnp.float32
BF16 = jnp.bfloat16
PARTS = 2
STRIP = 32
TILE = 256
LINE = 4
REACH = (1, 2, 4)
FAR_FIRST = (
    (8, 7, 9, 6, 10, 5, 11, 4, 12, 3, 13, 2, 14, 1, 15),
    (10, 6, 9, 7, 8, 11, 5, 2, 14, 3, 13, 12, 4, 1, 15),
)
OUT_ROWS = 96
OUT_STRIP = 32
VMEM_LIMIT = 34 * 1024 * 1024


def make_tables(count):
    index = np.arange(count)
    half = count // 2
    freq = np.where(index <= half, index, index - half)
    angle = 2.0 * np.pi / count * (freq[:, None] * index[None, :] % count)
    synth = np.where((index <= half)[:, None], np.cos(angle), np.sin(angle))
    weight = np.where((index == 0) | (index == half), 1.0 / count, 2.0 / count)
    analysis = weight[:, None] * synth
    as_bf16 = lambda table: jnp.asarray(table.astype(np.float32).astype(jnp.bfloat16))
    return as_bf16(synth), as_bf16(analysis)


def fold(value):
    total = None
    for row in range(0, value.shape[0], 8):
        for lane in range(0, value.shape[1], 128):
            piece = value[row : row + 8, lane : lane + 128]
            total = piece if total is None else total + piece
    return total


def dot(left, right):
    return jnp.dot(left, right, preferred_element_type=F32)


def steps_kernel(
    sizes, cells,
    v_hbm, couple_hbm, advect_ref, synth_k_hbm, anal_k_hbm, synth_m_hbm, anal_m_hbm,
    v_buf, w1_buf, spec, coef_ref,
    couple, synth_k, anal_k, synth_m, anal_m,
    sent_a, sent_b, low_a, high_a, next_a, low_b, high_b, next_b,
    relay_a, relay_b, mixed, inv_div, slots_one, slots_two,
    load_sem, v_sem,
    send_sem, recv_sem, hop_send, hop_recv, sum_send, sum_recv, met_sem,
):
    segs, rads, group = sizes
    chans, modes_m, modes_k = v_buf.shape
    rows = modes_m // PARTS
    pieces = [(c, q) for c in range(chans) for q in range(PARTS)]
    seg = lax.axis_index("seg")
    rad = lax.axis_index("rad")
    seg_prev = lax.rem(seg + segs - 1, segs)
    seg_next = lax.rem(seg + 1, segs)
    base = (seg // group) * group
    one_me = seg - base
    spread = segs // group
    two_count = spread * rads
    two_me = (seg // group) * rads + rad

    def one_peer(d):
        return lax.rem(one_me + d, group)

    def two_peer(d):
        other = lax.rem(two_me + d, two_count)
        return other, ((other // rads) * group + one_me, lax.rem(other, rads))

    upper_half = seg // group
    column, line = rad // LINE, lax.rem(rad, LINE)
    far_rad = (1 - column) * LINE + line
    detoured = ((line == LINE - 1) & (column == 0)) | ((line == 0) & (column == 1))
    is_source = (one_me == 0) & detoured
    is_sink = (one_me == group - 1) & detoured
    is_relay = (one_me == 1) & (((line == LINE - 1) & (column == 1)) | ((line == 0) & (column == 0)))
    relay = ((1 - upper_half) * group + 1, far_rad)
    relayed_source = ((1 - upper_half) * group, far_rad)
    relayed_sink = (base + group - 1, far_rad)

    barrier = pltpu.get_barrier_semaphore()

    def ring(which, offset):
        if which == 0:
            return base + lax.rem(one_me + group + offset, group), rad
        return two_peer(two_count + offset)[1]

    def signal(device):
        pl.semaphore_signal(barrier, inc=1, device_id=device, device_id_type=MESH)

    for which in (1, 0):
        signal(ring(which, 1))
        signal(ring(which, -1))
    for other in (seg_prev, seg_next):
        signal((other, rad))

    @pl.when(is_source)
    def _():
        signal(relay)

    @pl.when(is_sink)
    def _():
        signal((base + 1, far_rad))

    @pl.when(is_relay)
    def _():
        signal(relayed_source)
        signal(relayed_sink)

    loads = [
        pltpu.make_async_copy(source, target, load_sem.at[i])
        for i, (source, target) in enumerate(
            [
                (synth_k_hbm, synth_k),
                (synth_m_hbm, synth_m),
                (couple_hbm, couple),
                (anal_k_hbm, anal_k),
                (anal_m_hbm, anal_m),
            ]
        )
    ]
    v_loads = []
    for i, (c, q) in enumerate(pieces):
        at = (c, pl.ds(q * rows, rows))
        v_loads.append(pltpu.make_async_copy(v_hbm.at[at], v_buf.at[at], v_sem.at[i]))
        v_loads[-1].start()

    for load in loads:
        load.start()

    def say_met(step):
        for which in range(2):
            for offset in (REACH[step], -REACH[step]):
                pl.semaphore_signal(met_sem.at[which, step], inc=1, device_id=ring(which, offset), device_id_type=MESH)

    def wait_met(step):
        for which in range(2):
            pl.semaphore_wait(met_sem.at[which, step], 2)

    def sends(phase, i):
        c, q = pieces[i]
        at = (c, pl.ds(q * rows, rows))
        source = (sent_a, sent_b)[phase]
        low, high, nxt = ((low_a, high_a, next_a), (low_b, high_b, next_b))[phase]

        def copy(way, target, device):
            return pltpu.make_async_remote_copy(
                src_ref=source.at[at], dst_ref=target.at[at],
                send_sem=send_sem.at[phase, way, i], recv_sem=recv_sem.at[phase, way, i],
                device_id=device, device_id_type=MESH,
            )

        return (
            copy(0, low, (seg, lax.rem(rad + 1, rads))),
            copy(1, high, (seg, lax.rem(rad + rads - 1, rads))),
            copy(2, nxt, (seg_prev, rad)),
        )

    def hop(phase, i):
        c, q = pieces[i]
        at = (c, pl.ds(q * rows, rows))
        return pltpu.make_async_remote_copy(
            src_ref=(sent_a, sent_b)[phase].at[at], dst_ref=(relay_a, relay_b)[phase].at[at],
            send_sem=hop_send.at[phase, 0, i], recv_sem=hop_recv.at[phase, i],
            device_id=relay, device_id_type=MESH,
        )

    def onward(phase, i):
        c, q = pieces[i]
        at = (c, pl.ds(q * rows, rows))
        return pltpu.make_async_remote_copy(
            src_ref=(relay_a, relay_b)[phase].at[at], dst_ref=(next_a, next_b)[phase].at[at],
            send_sem=hop_send.at[phase, 1, i], recv_sem=recv_sem.at[phase, 2, i],
            device_id=relayed_sink, device_id_type=MESH,
        )

    def pass_on(phase, i):
        @pl.when(is_relay)
        def _():
            for j in ([0] if i == 0 else []) + ([i + 1] if i + 1 < len(pieces) else []):
                hop(phase, j).wait_recv()
                onward(phase, j).start()

    def start_sends(phase, i):
        up, down, back = sends(phase, i)

        @pl.when(rad < rads - 1)
        def _():
            up.start()

        @pl.when(rad > 0)
        def _():
            down.start()

        @pl.when(is_source)
        def _():
            hop(phase, i).start()

        @pl.when(jnp.logical_not(is_source))
        def _():
            back.start()

    def wait_recvs(phase, i):
        up, down, back = sends(phase, i)

        @pl.when(rad > 0)
        def _():
            up.wait_recv()

        @pl.when(rad < rads - 1)
        def _():
            down.wait_recv()

        back.wait_recv()

    def wait_sends(phase, i):
        up, down, back = sends(phase, i)

        @pl.when(rad < rads - 1)
        def _():
            up.wait_send()

        @pl.when(rad > 0)
        def _():
            down.wait_send()

        @pl.when(is_source)
        def _():
            hop(phase, i).wait_send()

        @pl.when(jnp.logical_not(is_source))
        def _():
            back.wait_send()

        @pl.when(is_relay)
        def _():
            onward(phase, i).wait_send()

    def strips(c, q, body, carry):
        def step(j, carry):
            row = pl.multiple_of(q * rows + j * STRIP, STRIP)
            return body(row, pl.ds(row, STRIP), carry)

        return lax.fori_loop(0, rows // STRIP, step, carry)

    zero = jnp.zeros((8, 128), F32)
    gram = [zero] * 6
    for i, (c, q) in enumerate(pieces):
        v_loads[i].wait()

        def rounding(row, at, total, c=c):
            value = v_buf[c, at, :]
            sent_a[c, at, :] = value.astype(BF16)
            return total + fold(value * value)

        gram[0] = strips(c, q, rounding, gram[0])
        if i == 0:
            extra = jnp.where(is_relay, 2, jnp.where(is_source | is_sink, 1, 0))
            pl.semaphore_wait(barrier, 6 + extra)
        start_sends(0, i)

    @pl.when(rad == 0)
    def _():
        low_a[...] = jnp.zeros_like(low_a)
        low_b[...] = jnp.zeros_like(low_b)

    @pl.when(rad == rads - 1)
    def _():
        high_a[...] = jnp.zeros_like(high_a)
        high_b[...] = jnp.zeros_like(high_b)

    say_met(0)

    def freq(index, count):
        return jnp.where(index <= count // 2, index, index - count // 2).astype(F32)

    freq_k = freq(lax.broadcasted_iota(jnp.int32, (1, modes_k), 1), modes_k)
    axial = VISC_AXIAL * (freq_k / (modes_k // 2)) ** 2
    mode = lax.broadcasted_iota(jnp.int32, (1, modes_k), 1)
    half = modes_k // 2
    wavenum = jnp.where(mode < half, mode, half - mode).astype(F32) * advect_ref[0]
    radius = (jnp.full((1, modes_k), rad + WINDOW_START, jnp.int32).astype(F32) + 0.5) / RADIAL_ALL

    def divide(j, _):
        row = pl.multiple_of(j * STRIP, STRIP)
        freq_m = freq(row + lax.broadcasted_iota(jnp.int32, (STRIP, modes_k), 0), modes_m)
        turning = (freq_m / (modes_m // 2)) ** 2
        inv_div[pl.ds(row, STRIP), :] = 1.0 / (1.0 + axial + VISC_TURN * turning / (radius * radius))
        return 0

    lax.fori_loop(0, modes_m // STRIP, divide, 0)

    def spectral(source):
        def synthesis(j, _):
            at = pl.ds(pl.multiple_of(j * TILE, TILE), TILE)
            physical = [
                dot(synth_m[...], dot(source[c], synth_k[:, at]).astype(BF16)) for c in range(chans)
            ]
            for c in range(chans):
                total = couple[c, 0, :, at].astype(F32) * physical[0]
                for k in range(1, chans):
                    total += couple[c, k, :, at].astype(F32) * physical[k]
                mixed[c, :, at] = total.astype(BF16)
            return 0

        lax.fori_loop(0, modes_k // TILE, synthesis, 0)

        def analysis(step, _):
            c = step // (modes_k // TILE)
            j = lax.rem(step, modes_k // TILE)
            at = pl.ds(pl.multiple_of(j * TILE, TILE), TILE)
            section = dot(mixed[c], anal_k[:, at]).astype(BF16)
            spec[c, :, at] = dot(anal_m[...], section)
            return 0

        lax.fori_loop(0, chans * (modes_k // TILE), analysis, 0)

    def image(field, bufs, c, at):
        sent, low, high, nxt = bufs
        swapped = jnp.concatenate([field[:, half:], field[:, :half]], axis=1)
        outer = low[c, at, :].astype(F32) + high[c, at, :].astype(F32)
        radial = RADIAL_GAIN * (outer - 2.0 * sent[c, at, :].astype(F32))
        total = field + spec[c, at, :] - wavenum * swapped + radial
        return total * inv_div[at, :] - nxt[c, at, :].astype(F32)

    for load in loads:
        load.wait()
    spectral(sent_a)
    wait_met(0)
    say_met(1)

    for i, (c, q) in enumerate(pieces):
        pass_on(0, i)
        wait_recvs(0, i)

        def first(row, at, totals, c=c):
            field = v_buf[c, at, :]
            value = image(field, (sent_a, low_a, high_a, next_a), c, at)
            w1_buf[c, at, :] = value
            sent_b[c, at, :] = value.astype(BF16)
            return totals[0] + fold(value * field), totals[1] + fold(value * value)

        gram[1], gram[2] = strips(c, q, first, (gram[1], gram[2]))
        start_sends(1, i)
        if i == 0:
            wait_met(1)
            say_met(2)
    wait_met(2)

    spectral(sent_b)

    for i, (c, q) in enumerate(pieces):
        pass_on(1, i)
        wait_sends(0, i)
        wait_recvs(1, i)

        def second(row, at, totals, c=c):
            field = w1_buf[c, at, :]
            value = image(field, (sent_b, low_b, high_b, next_b), c, at)
            spec[c, at, :] = value
            return (
                totals[0] + fold(value * v_buf[c, at, :]),
                totals[1] + fold(value * field),
                totals[2] + fold(value * value),
            )

        gram[3], gram[4], gram[5] = strips(c, q, second, (gram[3], gram[4], gram[5]))

    here = lax.broadcasted_iota(jnp.int32, (8, 128), 0) == lax.broadcasted_iota(jnp.int32, (8, 128), 1)
    rows_of = jnp.concatenate([jnp.sum(value, axis=0, keepdims=True) for value in gram] + [zero[:2]], axis=0)
    mine = jnp.sum(jnp.where(here, jnp.sum(rows_of, axis=1, keepdims=True), 0.0), axis=0, keepdims=True)
    stages = (
        (slots_one, one_me, group, lambda d: (base + one_peer(d), rad)),
        (slots_two, two_me, two_count, lambda d: two_peer(d)[1]),
    )

    def message(stage, d, slot):
        slots, _, _, peer = stages[stage]
        return pltpu.make_async_remote_copy(
            src_ref=slots.at[slot], dst_ref=slots.at[slot],
            send_sem=sum_send.at[stage, d], recv_sem=sum_recv.at[stage, d],
            device_id=peer(d), device_id_type=MESH,
        )

    def send_sums(stage, value):
        slots, me, _, _ = stages[stage]
        slots[me] = value
        for d in FAR_FIRST[stage]:
            message(stage, d, me).start()

    def total_of(stage):
        slots, me, count, _ = stages[stage]
        for d in FAR_FIRST[stage][::-1]:
            message(stage, d, lax.rem(me + count - d, count)).wait_recv()
        total = slots[0]
        for slot in range(1, count):
            total = total + slots[slot]
        return total

    def sums_sent(stage):
        for d in FAR_FIRST[stage]:
            message(stage, d, stages[stage][1]).wait_send()

    send_sums(0, mine)
    for i in range(len(pieces)):
        wait_sends(1, i)
    partial = total_of(0)
    send_sums(1, partial)
    sums_sent(0)
    sums = jnp.broadcast_to(total_of(1), (8, 128))
    sums = jnp.sum(jnp.where(here, sums, 0.0), axis=1, keepdims=True) * (1.0 / cells)
    sums = jnp.broadcast_to(sums, (8, 128))
    g00, g01, g11, g02, g12, g22 = (sums[i : i + 1] for i in range(6))
    start_norm = jnp.sqrt(g00)
    upper_one = g01 / g00
    lower_one = jnp.sqrt(g11 / g00 - upper_one * upper_one)
    scale = start_norm * lower_one
    upper_two = (g02 - upper_one * g01) / (g00 * lower_one)
    middle_two = (g12 - upper_one * (g02 + g11) + upper_one * upper_one * g01) / (scale * scale)
    length = (g22 - 2.0 * upper_one * g12 + upper_one * upper_one * g11) / (scale * scale)
    lower_two = jnp.sqrt(length - upper_two * upper_two - middle_two * middle_two)
    on_two = 1.0 / (scale * lower_two)
    on_one = -(upper_one + middle_two) * on_two
    on_start = (middle_two * upper_one / scale - upper_two / start_norm) / lower_two
    coef_ref[0:8, :] = jnp.concatenate(
        [start_norm, upper_one, lower_one, upper_two, middle_two, lower_two, on_two, on_one], axis=0
    )
    coef_ref[8:16, :] = jnp.broadcast_to(on_start, (8, 128))

    sums_sent(1)


def combine_kernel(coef_ref, v_ref, w1_ref, w2_ref, out_ref, hess_ref, stage, sem):
    chans, modes_m, modes_k = v_ref.shape
    on_two = jnp.broadcast_to(coef_ref[6:7, 0:1], (OUT_STRIP, modes_k))
    on_one = jnp.broadcast_to(coef_ref[7:8, 0:1], (OUT_STRIP, modes_k))
    on_start = jnp.broadcast_to(coef_ref[8:9, 0:1], (OUT_STRIP, modes_k))
    pieces = [(c, row) for c in range(chans) for row in range(0, modes_m, OUT_ROWS)]

    def copy(i):
        c, row = pieces[i]
        at = (c, pl.ds(row, OUT_ROWS))
        return pltpu.make_async_copy(stage.at[at], out_ref.at[at], sem.at[i])

    for i, (c, row) in enumerate(pieces):

        def strip(j, _, c=c, row=row):
            at = pl.ds(pl.multiple_of(row + j * OUT_STRIP, OUT_STRIP), OUT_STRIP)
            stage[c, at, :] = (
                on_two * w2_ref[c, at, :] + on_one * w1_ref[c, at, :] + on_start * v_ref[c, at, :]
            )
            return 0

        lax.fori_loop(0, OUT_ROWS // OUT_STRIP, strip, 0)
        copy(i).start()
    for i in range(6):
        hess_ref[i] = coef_ref[i, 0]
    for i in range(len(pieces)):
        copy(i).wait()


def on_device(segs, rads, start_vector, coupling, advect):
    shape = start_vector.shape
    chans, modes_m, modes_k = shape[1], shape[3], shape[4]
    vector = start_vector.reshape(chans, modes_m, modes_k)
    couple = coupling.reshape(chans, chans, modes_m, modes_k)
    cells = float(segs * rads * chans * modes_m * modes_k)
    synth_m, anal_m = make_tables(modes_m)
    synth_k, anal_k = make_tables(modes_k)
    group = 16
    two_count = (segs // group) * rads
    field = (chans, modes_m, modes_k)
    count = chans * PARTS
    in_place = lambda value: pltpu.with_memory_space_constraint(value, pltpu.HBM)
    tables = (synth_k, anal_k.T, synth_m.T, anal_m)
    in_hbm = pl.BlockSpec(memory_space=pltpu.HBM)
    in_vmem = pl.BlockSpec(memory_space=pltpu.VMEM)
    v, w1, w2, coef = pl.pallas_call(
        functools.partial(steps_kernel, (segs, rads, group), cells),
        out_shape=[jax.ShapeDtypeStruct(field, F32)] * 3 + [jax.ShapeDtypeStruct((16, 128), F32)],
        in_specs=[in_hbm, in_hbm, pl.BlockSpec(memory_space=pltpu.SMEM)] + [in_hbm] * 4,
        out_specs=[in_vmem] * 4,
        scratch_shapes=[
            pltpu.VMEM((chans,) + field, BF16),
            pltpu.VMEM((modes_k, modes_k), BF16),
            pltpu.VMEM((modes_k, modes_k), BF16),
            pltpu.VMEM((modes_m, modes_m), BF16),
            pltpu.VMEM((modes_m, modes_m), BF16),
        ]
        + [pltpu.VMEM(field, BF16)] * 11
        + [
            pltpu.VMEM((modes_m, modes_k), F32),
            pltpu.VMEM((group, 1, 128), F32),
            pltpu.VMEM((two_count, 1, 128), F32),
            pltpu.SemaphoreType.DMA((5,)),
            pltpu.SemaphoreType.DMA((count,)),
            pltpu.SemaphoreType.DMA((2, 3, count)),
            pltpu.SemaphoreType.DMA((2, 3, count)),
            pltpu.SemaphoreType.DMA((2, 2, count)),
            pltpu.SemaphoreType.DMA((2, count)),
            pltpu.SemaphoreType.DMA((2, 16)),
            pltpu.SemaphoreType.DMA((2, 16)),
            pltpu.SemaphoreType.REGULAR((2, len(REACH))),
        ],
        compiler_params=pltpu.CompilerParams(
            collective_id=0, has_side_effects=True, vmem_limit_bytes=VMEM_LIMIT
        ),
    )(in_place(vector), in_place(couple), advect, *map(in_place, tables))
    out, hess = pl.pallas_call(
        combine_kernel,
        out_shape=(jax.ShapeDtypeStruct(field, F32), jax.ShapeDtypeStruct((6,), F32)),
        in_specs=[in_vmem] * 4,
        out_specs=(in_hbm, pl.BlockSpec(memory_space=pltpu.SMEM)),
        scratch_shapes=[
            pltpu.VMEM(field, F32),
            pltpu.SemaphoreType.DMA((chans * modes_m // OUT_ROWS,)),
        ],
        compiler_params=pltpu.CompilerParams(vmem_limit_bytes=VMEM_LIMIT),
    )(coef, v, w1, w2)
    return out.reshape(shape), hess


def solution(mesh):
    return jax.shard_map(
        functools.partial(on_device, mesh.shape["seg"], mesh.shape["rad"]),
        mesh=mesh,
        in_specs=(
            P("seg", None, "rad", None, None),
            P("seg", None, None, "rad", None, None),
            P("rad"),
        ),
        out_specs=(P("seg", None, "rad", None, None), P()),
        check_vma=False,
    )
```
